32 devices in a mesh: patch: 16 (over z, y, core), seq: 2 (over x).
Axes of the slice: x: 2, y: 2, z: 4, core: 2. Of those that a mesh axis runs over, the one named last changes fastest.
Arguments:
- tokens: bfloat16 [2, 16, 256, 1152], P('seq', None, 'patch'), may hold values from -6 to 6
- cotangent: bfloat16 [2, 16, 256, 1152], P('seq', None, 'patch'), may hold values from -6 to 6
- class_ids: int32 [2], P('seq'), may hold values from 0 to 100
- timesteps: int32 [2], P('seq'), may hold values from 0 to 999
- segments: int32 [2, 16], P('seq'), may hold values from 0 to 3, never falling along the last dimension, each value on 1 to 8 neighbouring positions
- class_table: bfloat16 [101, 1152], replicated, may hold values from -6 to 6
- mod_spatial: bfloat16 [1152, 6912], P('patch', 'seq'), may hold values from -0.1875 to 0.1875
- qkv_spatial: bfloat16 [1152, 3456], P('patch', 'seq'), may hold values from -0.1875 to 0.1875
- out_spatial: bfloat16 [1152, 1152], P('patch', 'seq'), may hold values from -2 to 2
- up_spatial: bfloat16 [1152, 4608], P('patch', 'seq'), may hold values from -0.1875 to 0.1875
- down_spatial: bfloat16 [4608, 1152], P('patch', 'seq'), may hold values from -0.125 to 0.125
- mod_temporal: bfloat16 [1152, 6912], P('patch', 'seq'), may hold values from -0.1875 to 0.1875
- qkv_temporal: bfloat16 [1152, 3456], P('patch', 'seq'), may hold values from -0.1875 to 0.1875
- out_temporal: bfloat16 [1152, 1152], P('patch', 'seq'), may hold values from -0.375 to 0.375
- up_temporal: bfloat16 [1152, 4608], P('patch', 'seq'), may hold values from -0.1875 to 0.1875
- down_temporal: bfloat16 [4608, 1152], P('patch', 'seq'), may hold values from -0.125 to 0.125
Outputs:
- out_tokens: bfloat16 [2, 16, 256, 1152], P('seq', None, 'patch')
- grad_tokens: float32 [2, 16, 256, 1152], P('seq', None, 'patch')
- grad_class_table: float32 [101, 1152], replicated
- grad_mod_spatial: float32 [1152, 6912], P('patch', 'seq')
- grad_qkv_spatial: float32 [1152, 3456], P('patch', 'seq')
- grad_out_spatial: float32 [1152, 1152], P('patch', 'seq')
- grad_up_spatial: float32 [1152, 4608], P('patch', 'seq')
- grad_down_spatial: float32 [4608, 1152], P('patch', 'seq')
- grad_mod_temporal: float32 [1152, 6912], P('patch', 'seq')
- grad_qkv_temporal: float32 [1152, 3456], P('patch', 'seq')
- grad_out_temporal: float32 [1152, 1152], P('patch', 'seq')
- grad_up_temporal: float32 [1152, 4608], P('patch', 'seq')
- grad_down_temporal: float32 [4608, 1152], P('patch', 'seq')
The draws below stay inside these ranges and needn't reach their ends.
Inputs may be any that keep to these rules, and one draw needn't show every extreme that they name: `segments`: along the frame slots of a sequence the clip numbers never fall; every clip number occurs, each clip holds 1 to 8 slots, and one holds exactly 8.
All inputs are finite; a program needn't handle non-finite values.
Results may differ from the reference program's by a relative error of at most 0.02.
Values may be sent and summed in bfloat16 or wider, within the bound.
No kernel may reach another device: no remote copies, remote signals or barrier semaphores. Data moves between devices by JAX's collectives and lax.ppermute only.
A program may use at most 384 MiB of HBM per device.

```python
import math
import jax
import jax.numpy as jnp
import numpy as np
from jax import lax

D = 1152
HEADS = 16
FF = 4608
CLASSES = 101
PATCHES = 256
FRAMES = 16
CLIPS = 4
STEPS = 1000
SEQS = 2


def steps_of(key, shape, cuts, least, largest):
    def one(dim, blocks):
        steps = jax.random.uniform(jax.random.fold_in(jax.random.fold_in(key, 6), dim), (blocks,), jnp.float32, least / len(cuts), largest / len(cuts))
        return jnp.repeat(jnp.exp(steps), shape[dim] // blocks).reshape((-1,) + (1,) * (len(shape) - dim - 1))

    loudness = one(*cuts[0])
    for cut in cuts[1:]:
        loudness = loudness * one(*cut)
    return loudness


def length_profile(number_of, total, most, skew):
    portions = [(1 << 20) // math.isqrt(standing ** skew) + 1 for standing in range(2, number_of + 1)]
    surplus, counts = total - most - (number_of - 1), [1] * (number_of - 1)
    while surplus > 0:
        candidates = [i for i in range(number_of - 1) if counts[i] < most]
        whole, budget = sum([portions[i] for i in candidates]), surplus
        for i in candidates:
            more = min(most - counts[i], max(1, budget * portions[i] // whole), surplus)
            counts[i] = counts[i] + more
            surplus = surplus - more
    return np.array([most] + counts)


def ragged_sizes(key, number_of, total, bound, skew):
    if number_of == 2:
        one = jax.random.randint(key, (), max(1, total - bound), min(bound, total - 1) + 1)
        return jnp.stack([one, total - one])
    tallies = jnp.asarray(length_profile(number_of, total, bound, skew), jnp.int32)
    pairs = (number_of - 1) // 2
    donor, taker = tallies[1:1 + 2 * pairs:2], tallies[2:2 + 2 * pairs:2]
    margin = jnp.minimum(donor - 1, bound - taker)
    passed = jax.random.randint(jax.random.fold_in(key, 1), (pairs,), 0, 1 << 20) % (margin + 1)
    tallies = tallies.at[1:1 + 2 * pairs:2].set(donor - passed).at[2:2 + 2 * pairs:2].set(taker + passed)
    return tallies[jax.random.permutation(jax.random.fold_in(key, 2), number_of)]


def normal_values(rng, dims, width, most, cuts=(), held_as=jnp.bfloat16):
    values = width * jax.random.normal(rng, dims, jnp.float32)
    if cuts:
        values = values * steps_of(rng, dims, cuts, -0.22, 0.18)
    return jnp.clip(values, -most, most).astype(held_as)


def setup_inputs(seed: int = 0) -> dict:
    key_of = jax.random.split(jax.random.key(seed), 17)
    return {
        "tokens": normal_values(key_of[0], (SEQS, FRAMES, PATCHES, D), 1.0, 6.0, ((0, 2), (2, 16))),
        "cotangent": normal_values(key_of[1], (SEQS, FRAMES, PATCHES, D), 1.0, 6.0, ((0, 2), (2, 16))),
        "class_ids": jax.random.randint(key_of[2], (SEQS,), 0, CLASSES).astype(jnp.int32),
        "timesteps": jax.random.randint(key_of[3], (SEQS,), 0, STEPS).astype(jnp.int32),
        "segments": jax.vmap(lambda own: jnp.searchsorted(jnp.cumsum(ragged_sizes(own, CLIPS, FRAMES, FRAMES // 2, 1)), jnp.arange(FRAMES), side="right"))(jax.random.split(key_of[4], SEQS)).reshape((SEQS, FRAMES)).astype(jnp.int32),
        "class_table": normal_values(key_of[5], (CLASSES, D), 1.0, 6.0),
        "mod_spatial": normal_values(key_of[6], (D, 6 * D), D ** -0.5, 0.1875, ((0, 16), (1, 2))),
        "qkv_spatial": normal_values(key_of[7], (D, 3 * D), D ** -0.5, 0.1875, ((0, 16), (1, 2))),
        "out_spatial": normal_values(key_of[8], (D, D), (max(D // 128, 1)) ** -0.5, 2.0, ((0, 16), (1, 2))),
        "up_spatial": normal_values(key_of[9], (D, FF), D ** -0.5, 0.1875, ((0, 16), (1, 2))),
        "down_spatial": normal_values(key_of[10], (FF, D), (FF // 2) ** -0.5, 0.125, ((0, 16), (1, 2))),
        "mod_temporal": normal_values(key_of[11], (D, 6 * D), D ** -0.5, 0.1875, ((0, 16), (1, 2))),
        "qkv_temporal": normal_values(key_of[12], (D, 3 * D), D ** -0.5, 0.1875, ((0, 16), (1, 2))),
        "out_temporal": normal_values(key_of[13], (D, D), (D // 4) ** -0.5, 0.375, ((0, 16), (1, 2))),
        "up_temporal": normal_values(key_of[14], (D, FF), D ** -0.5, 0.1875, ((0, 16), (1, 2))),
        "down_temporal": normal_values(key_of[15], (FF, D), (FF // 2) ** -0.5, 0.125, ((0, 16), (1, 2))),
    }


@jax.custom_vjp
def low(v):
    return lax.optimization_barrier(v.astype(jnp.bfloat16)).astype(jnp.float32)

@jax.custom_vjp
def low_back(v):
    return v

def low_keep(v):
    return (low(v), None)

def low_pass(kept, grad):
    return (grad,)

def back_keep(v):
    return (v, None)

def back_low(kept, grad):
    return (low(grad),)
low.defvjp(low_keep, low_pass)
low_back.defvjp(back_keep, back_low)
PRECISE = lax.Precision.HIGHEST

def product(left, right):
    return jnp.dot(left, right, precision=PRECISE)

def layer_norm(values):
    centred = values - lax.optimization_barrier(jnp.mean(values, axis=-1, keepdims=True))
    variance = lax.optimization_barrier(jnp.mean(centred * centred, axis=-1, keepdims=True))
    return centred * lax.rsqrt(variance + 1e-06)

def time_features(step_ids, features):
    half_width = features // 2
    frequency = jnp.exp(-math.log(10000.0) * jnp.arange(half_width, dtype=jnp.float32) / half_width)
    angles = step_ids.astype(jnp.float32)[:, None] * frequency[None, :]
    return jnp.concatenate([jnp.cos(angles), jnp.sin(angles)], axis=-1)

def split_heads(values):
    return values.reshape(values.shape[:-1] + (HEADS, values.shape[-1] // HEADS))

def spatial_mix(qkv_block):
    features = qkv_block.shape[-1] // 3
    queries = split_heads(qkv_block[..., :features])
    keys_all = split_heads(qkv_block[..., features:2 * features])
    values = split_heads(qkv_block[..., 2 * features:])
    factor = (features // HEADS) ** (-0.5)
    scores = low_back(jnp.einsum('fphd,fkhd->fhpk', queries, keys_all, precision=PRECISE) * factor)
    weights = low(jax.nn.softmax(scores, axis=-1))
    mixture = jnp.einsum('fhpk,fkhd->fphd', weights, values, precision=PRECISE)
    return mixture.reshape(qkv_block.shape[:-1] + (features,))

def temporal_mix(qkv_block, same_clip):
    features = qkv_block.shape[-1] // 3
    queries = split_heads(qkv_block[..., :features])
    keys_all = split_heads(qkv_block[..., features:2 * features])
    values = split_heads(qkv_block[..., 2 * features:])
    factor = (features // HEADS) ** (-0.5)
    scores = low_back(jnp.einsum('fphd,gphd->phfg', queries, keys_all, precision=PRECISE) * factor)
    scores = jnp.where(same_clip[None, None, :, :], scores, -1e+30)
    weights = low(jax.nn.softmax(scores, axis=-1))
    mixture = jnp.einsum('phfg,gphd->fphd', weights, values, precision=PRECISE)
    return mixture.reshape(qkv_block.shape[:-1] + (features,))

def layer_block(residual, modulation, matrices, attend):
    qkv_weight, out_weight, up_weight, down_weight = matrices
    features = residual.shape[-1]
    pieces = [modulation[number * features:(number + 1) * features] for number in range(6)]
    flat_rows = residual.reshape(-1, features)
    hidden_one = low(layer_norm(flat_rows) * (1.0 + pieces[1]) + pieces[0])
    qkv_rows = low(low_back(product(hidden_one, qkv_weight)))
    attended = attend(qkv_rows.reshape(residual.shape[0], residual.shape[1], 3 * features))
    attended = low(low_back(attended.reshape(-1, features)))
    branch = low_back(product(attended, out_weight))
    middle = flat_rows + pieces[2] * branch
    hidden_two = low(layer_norm(middle) * (1.0 + pieces[4]) + pieces[3])
    pre_gelu = low_back(product(hidden_two, up_weight))
    activated = low(jax.nn.gelu(pre_gelu, approximate=True))
    mlp_output = low_back(product(activated, down_weight))
    return (middle + pieces[5] * mlp_output).reshape(residual.shape)

def reference(tokens, cotangent, class_ids, timesteps, segments, class_table, mod_spatial, qkv_spatial, out_spatial, up_spatial, down_spatial, mod_temporal, qkv_temporal, out_temporal, up_temporal, down_temporal):
    matrices = [weight.astype(jnp.float32) for weight in (mod_spatial, qkv_spatial, out_spatial, up_spatial, down_spatial, mod_temporal, qkv_temporal, out_temporal, up_temporal, down_temporal)]
    one_hot = (class_ids[:, None] == jnp.arange(CLASSES, dtype=jnp.int32)[None, :]).astype(jnp.float32)
    time_rows = time_features(timesteps, D)
    same_clip = segments[:, :, None] == segments[:, None, :]

    def forward(residual, table, *weights):
        condition = product(one_hot, table) + time_rows
        cond_low = low(jax.nn.silu(condition))
        spatial_mods = product(cond_low, weights[0])
        temporal_mods = product(cond_low, weights[5])

        def one_sequence(item):
            sequence, mods_one, mods_two, clip_table = item
            middle = layer_block(sequence, mods_one, weights[1:5], spatial_mix)
            return layer_block(middle, mods_two, weights[6:10], lambda qkv_block: temporal_mix(qkv_block, clip_table))
        return lax.map(jax.checkpoint(one_sequence), (residual, spatial_mods, temporal_mods, same_clip))
    result, pullback = jax.vjp(forward, tokens.astype(jnp.float32), class_table.astype(jnp.float32), *matrices)
    grads = pullback(cotangent.astype(jnp.float32))
    return (result.astype(jnp.bfloat16), grads[0], grads[1], grads[2], grads[3], grads[4], grads[5], grads[6], grads[7], grads[8], grads[9], grads[10], grads[11])
```

```python
import math
from functools import partial

import jax
import jax.numpy as jnp
from jax import lax
from jax.experimental import pallas as pl
from jax.experimental.pallas import tpu as pltpu
from jax.sharding import Mesh
from jax.sharding import PartitionSpec as P

HEADS = 16
EPSILON = 1e-06
PRECISE = lax.Precision.HIGHEST
LOW = jnp.bfloat16
FULL = jnp.float32


def time_features(step_ids, features):
    half_width = features // 2
    frequency = jnp.exp(-math.log(10000.0) * jnp.arange(half_width, dtype=FULL) / half_width)
    angles = step_ids.astype(FULL)[:, None] * frequency[None, :]
    return jnp.concatenate([jnp.cos(angles), jnp.sin(angles)], axis=-1)


def normalize(values):
    centred = values - jnp.mean(values, axis=-1, keepdims=True)
    inverse = lax.rsqrt(jnp.mean(centred * centred, axis=-1, keepdims=True) + EPSILON)
    return centred * inverse, inverse


def normalize_back(grad_norm, normed, inverse):
    return inverse * (
        grad_norm
        - jnp.mean(grad_norm, axis=-1, keepdims=True)
        - normed * jnp.mean(grad_norm * normed, axis=-1, keepdims=True)
    )


def matmul(left, right):
    return jnp.dot(left, right, preferred_element_type=FULL)


def matmul_nt(left, right):
    return lax.dot_general(left, right, (((1,), (1,)), ((), ())), preferred_element_type=FULL)


def matmul_tn(left, right):
    return lax.dot_general(left, right, (((0,), (0,)), ((), ())), preferred_element_type=FULL)


def in_order(pieces, first):
    count = len(pieces)
    return [lax.select_n((k - first) % count, *pieces) for k in range(count)]


def pick(array, axis, index):
    return lax.dynamic_index_in_dim(array, index, axis, keepdims=False)


LIMIT = 60 * 2**20
CHIPS_Y = 2


def at_rows(index, rows):
    return pl.ds(pl.multiple_of(index * rows, 16), rows)


class Weight:
    def __init__(self, depth, rows, cols, strips):
        self.depth, self.rows, self.cols, self.strips = depth, rows, cols, strips
        self.width = -(-cols // 128) * 128 if strips[0][1] is None else cols
        self.arrays = []
        for strip in strips:
            for array in strip[0]:
                if not any(array is other for other in self.arrays):
                    self.arrays.append(array)

    def scratch(self):
        return [
            pltpu.VMEM((2, 2, 2 * self.depth * self.rows, self.width), LOW),
            pltpu.SemaphoreType.DMA((2, 2, 2, self.depth * len(self.strips))),
        ]

    def copies(self, where, refs, held, sems):
        found = []
        for half in range(2):
            for side in range(2):
                group = []
                x = lax.rem(where[3] + side, 2)
                for turn in range(2):
                    y = lax.rem(where[1] + turn, 2)
                    for ahead in range(self.depth):
                        z = lax.rem(where[0] + ahead, self.depth)
                        at = (z * CHIPS_Y + y) * self.rows
                        base = 0
                        for number, strip in enumerate(self.strips):
                            arrays, x_first, source_lane, row, rows, lane, lanes = strip
                            if x_first is None:
                                core = lax.rem(where[2] + half, 2)
                                source = refs[0].at[
                                    z, y, core, x, :, source_lane : source_lane + lanes
                                ]
                            else:
                                first, second = (side, turn) if x_first else (turn, side)
                                source = refs[base + 2 * half + second].at[first, ahead]
                                base += 4
                            start = pl.multiple_of(at + row, 16)
                            target = held.at[half, x, pl.ds(start, rows), lane : lane + lanes]
                            sem = sems.at[half, side, turn, ahead * len(self.strips) + number]
                            group.append(pltpu.make_async_copy(source, target, sem))
                found.append(group)
        return found


def start_all(copies):
    for copy in copies:
        copy.start()


def wait_all(copies):
    for copy in copies:
        copy.wait()


def dot(left, right):
    return lax.dot_general(left, right, (((1,), (0,)), ((), ())), preferred_element_type=FULL)


def dot_nt(left, right):
    return lax.dot_general(left, right, (((1,), (1,)), ((), ())), preferred_element_type=FULL)


def dot_tn(left, right):
    return lax.dot_general(left, right, (((0,), (0,)), ((), ())), preferred_element_type=FULL)


def call(body, where, ins, outs, scratch, flops, name, after=()):
    count = len(ins)

    def kernel(where_ref, *refs):
        body(where_ref, *refs[:count], *refs[count + len(after) :])

    vmem = pl.BlockSpec(memory_space=pltpu.VMEM)
    hbm = pl.BlockSpec(memory_space=pl.ANY)
    size = sum(a.size * a.dtype.itemsize for a, _ in ins)
    size += sum(math.prod(o.shape) * o.dtype.itemsize for o in outs)
    return pl.pallas_call(
        kernel,
        out_shape=outs,
        in_specs=[pl.BlockSpec(memory_space=pltpu.SMEM)]
        + [vmem if inside else hbm for _, inside in ins]
        + [hbm] * len(after),
        out_specs=[vmem] * len(outs),
        scratch_shapes=scratch,
        compiler_params=pltpu.CompilerParams(vmem_limit_bytes=LIMIT),
        cost_estimate=pl.CostEstimate(flops=flops, bytes_accessed=size, transcendentals=0),
        name=name,
    )(where, *[a for a, _ in ins], *after)


def shape(dims, dtype):
    return jax.ShapeDtypeStruct(dims, dtype)


def norm_qkv(where, rows, mods, weight, cols):
    count, features = rows.shape
    many = len(weight.arrays)
    thin = weight.cols - cols
    chips = 2 * weight.depth
    part = weight.rows // 2

    def body(where, rows, mods, *refs):
        sources, (hidden, out_weight, out, held, sems) = refs[:many], refs[many:]
        copies = weight.copies(where, sources, held, sems)
        for group in copies:
            start_all(group)
        normed, _ = normalize(rows[...].astype(FULL))
        value = (normed * (1.0 + mods[1:2]) + mods[0:1]).astype(LOW)
        hidden[...] = value
        for half in range(2):
            for side in range(2):
                x = lax.rem(where[3] + side, 2)
                wait_all(copies[2 * half + side])
                out[2 * half + x] = dot(value, held[half, x, :, :cols]).astype(LOW)
                strips = held[half, x, :, cols:].astype(FULL).reshape(chips, 2, part, thin)
                both = [strips[:, k].reshape(chips * part, thin) for k in range(2)]
                out_weight[2 * half + x] = jnp.concatenate(both, axis=1).astype(LOW)

    return call(
        body,
        where,
        [(rows, True), (mods, True)] + [(w, False) for w in weight.arrays],
        [
            shape((count, features), LOW),
            shape((4, chips * part, 2 * thin), LOW),
            shape((4, count, cols), LOW),
        ],
        weight.scratch(),
        8 * count * features * cols,
        "norm_qkv",
    )


def head_slices(qkv, half, number, heads, head):
    def column(slot):
        per = 3 * heads // 2
        x, at = divmod(slot, per)
        return qkv[2 * half + x, :, at * head : (at + 1) * head]

    return column(number), column(heads + number), column(2 * heads + number)


def probabilities(query, key, mask, factor):
    scores = dot_nt(key, query) * factor
    if mask is not None:
        scores = jnp.where(mask, scores, -1e30)
    weights = jnp.exp(scores - jnp.max(scores, axis=0, keepdims=True))
    return weights * (1.0 / jnp.sum(weights, axis=0, keepdims=True))


def attend_kernel(where, qkv, marks, head):
    _, count, cols = qkv.shape
    heads = 2 * cols // (3 * head)

    def body(where, qkv, *refs):
        mask = None
        if marks is not None:
            mask = refs[0][...] == refs[1][...]
        out = refs[-1]
        for half in range(2):
            mixed = []
            for number in range(heads):
                query, key, value = head_slices(qkv, half, number, heads, head)
                probs = probabilities(query, key, mask, head ** (-0.5)).astype(LOW)
                mixed.append(dot_tn(value, probs))
            out[half] = jnp.concatenate(mixed, axis=0).T.astype(LOW)

    ins = [(qkv, True)] + ([] if marks is None else [(m, True) for m in marks])
    return call(
        body,
        where,
        ins,
        [shape((2, count, heads * head), LOW)],
        [],
        8 * heads * count * count * head,
        "attend",
    )[0]


def out_norm(where, rows, mods, attended, weight):
    count, features = rows.shape

    def body(where, rows, mods, attended, weight, branch, middle, hidden):
        value = jnp.concatenate(
            [dot(attended[0], weight[x]) + dot(attended[1], weight[2 + x]) for x in range(2)],
            axis=1,
        )
        branch[...] = value
        total = rows[...].astype(FULL) + mods[2:3] * value
        middle[...] = total
        normed, _ = normalize(total)
        hidden[...] = (normed * (1.0 + mods[4:5]) + mods[3:4]).astype(LOW)

    dims = (count, features)
    return call(
        body,
        where,
        [(rows, True), (mods, True), (attended, True), (weight, True)],
        [shape(dims, FULL), shape(dims, FULL), shape(dims, LOW)],
        [],
        2 * count * features * features,
        "out_norm",
    )


GELU_A = math.sqrt(2.0 / math.pi)
GELU_B = 0.044715


def gelu(value):
    inner = GELU_A * (value + GELU_B * value * value * value)
    return 0.5 * value * (1.0 + jnp.tanh(inner))


def gelu_slope(value):
    square = value * value
    bend = jnp.tanh(GELU_A * (value + GELU_B * square * value))
    return 0.5 * (1.0 + bend) + 0.5 * value * (1.0 - bend * bend) * GELU_A * (
        1.0 + 3.0 * GELU_B * square
    )


def up_gelu(where, hidden, weight):
    count, features = hidden.shape
    cols, many = weight.cols, len(weight.arrays)

    def body(where, hidden, *refs):
        sources, (pre, act, held, sems) = refs[:many], refs[many:]
        copies = weight.copies(where, sources, held, sems)
        for group in copies:
            start_all(group)
        value = hidden[...]
        for half in range(2):
            for side in range(2):
                x = lax.rem(where[3] + side, 2)
                wait_all(copies[2 * half + side])
                before = dot(value, held[half, x])
                pre[2 * half + x] = before.astype(LOW)
                act[2 * half + x] = gelu(before).astype(LOW)

    return call(
        body,
        where,
        [(hidden, True)] + [(w, False) for w in weight.arrays],
        [shape((4, count, cols), LOW), shape((4, count, cols), LOW)],
        weight.scratch(),
        8 * count * features * cols,
        "up_gelu",
    )


def by_place(first, pair):
    return [jnp.where(first, pair[0], pair[1]), jnp.where(first, pair[1], pair[0])]


def down_add(where, act, weight, middle, mods):
    count, features = middle.shape
    wide, many = act.shape[-1], len(weight.arrays)

    def body(where, act, middle, mods, *refs):
        sources, (mlp, out, held, sems) = refs[:many], refs[many:]
        copies = weight.copies(where, sources, held, sems)
        for group in copies:
            start_all(group)
        totals = [None, None]
        for half in range(2):
            for side in range(2):
                place = lax.rem(where[3] + side, 2)
                wait_all(copies[2 * half + side])
                for x in range(2):
                    part = dot(act[2 * half + x], held[half, place, x * wide : (x + 1) * wide])
                    totals[side] = part if totals[side] is None else totals[side] + part
        sides = by_place(where[3] == 0, [t[:, : weight.cols] for t in totals])
        total = jnp.concatenate(sides, axis=1)
        mlp[...] = total
        out[...] = (middle[...] + mods[5:6] * total).astype(LOW)

    return call(
        body,
        where,
        [(act, True), (middle, True), (mods, True)] + [(w, False) for w in weight.arrays],
        [shape((count, features), FULL), shape((count, features), LOW)],
        weight.scratch(),
        8 * count * features * wide,
        "down_add",
    )


def column_sums(*values):
    sums = [jnp.sum(v, axis=0, keepdims=True) for v in values]
    fill = jnp.zeros((8 - len(sums), sums[0].shape[1]), FULL)
    return jnp.concatenate(sums + [fill], axis=0)


def mlp_back(where, grad, mods, pre, middle, branch, mlp, up, down):
    count, features = grad.shape
    wide = pre.shape[-1]
    cols = down.cols
    many_up, many_down = len(up.arrays), len(down.arrays)
    shared = up.arrays[0] is down.arrays[0]

    def body(where, grad, mods, pre, middle, branch, mlp, *refs):
        ups = refs[:many_up]
        refs = refs[many_up:]
        downs = ups
        if not shared:
            downs, refs = refs[:many_down], refs[many_down:]
        grad_mid, grad_pre, grad_branch, sums, up_held, up_sems, down_held, down_sems = refs
        down_copies = down.copies(where, downs, down_held, down_sems)
        up_copies = up.copies(where, ups, up_held, up_sems)
        for half in range(2):
            start_all(down_copies[2 * half])
            start_all(down_copies[2 * half + 1])
            start_all(up_copies[2 * half])
            start_all(up_copies[2 * half + 1])
        incoming = grad[...].astype(FULL)
        grad_mlp = (mods[5:6] * incoming).astype(LOW)
        sides = [grad_mlp[:, s * cols : (s + 1) * cols] for s in range(2)]
        total = None
        for half in range(2):
            wait_all(down_copies[2 * half] + down_copies[2 * half + 1])
            for side in range(2):
                x = lax.rem(where[3] + side, 2)
                rows = pl.ds(pl.multiple_of(x * wide, 16), wide)
                grad_act = dot_nt(sides[0], down_held[half, 0, rows, :cols]) + dot_nt(
                    sides[1], down_held[half, 1, rows, :cols]
                )
                slope = gelu_slope(pre[2 * half + x].astype(FULL))
                value = (slope * grad_act).astype(LOW)
                grad_pre[2 * half + x] = value
                wait_all(up_copies[2 * half + side])
                part = dot_nt(value, up_held[half, x])
                total = part if total is None else total + part
        normed, inverse = normalize(middle[...])
        result = incoming + normalize_back(total * (1.0 + mods[4:5]), normed, inverse)
        grad_mid[...] = result
        scaled = (mods[2:3] * result).astype(LOW)
        for s in range(2):
            grad_branch[s] = scaled[:, s * cols : (s + 1) * cols]
        sums[...] = column_sums(result * branch[...], total, total * normed, incoming * mlp[...])

    arrays = up.arrays + ([] if shared else down.arrays)
    return call(
        body,
        where,
        [(a, True) for a in (grad, mods, pre, middle, branch, mlp)] + [(w, False) for w in arrays],
        [
            shape((count, features), FULL),
            shape(pre.shape, LOW),
            shape((2, count, cols), LOW),
            shape((8, features), FULL),
        ],
        up.scratch() + down.scratch(),
        16 * count * features * wide,
        "mlp_back",
    )


def scale_halves(where, grad, mods):
    count, features = grad.shape

    def body(where, grad, mods, out):
        value = (mods[5:6] * grad[...].astype(FULL)).astype(LOW)
        for side in range(2):
            out[side] = value[:, side * features // 2 : (side + 1) * features // 2]

    return call(
        body,
        where,
        [(grad, True), (mods, True)],
        [shape((2, count, features // 2), LOW)],
        [],
        0,
        "scale_halves",
    )[0]


def attend_back_kernel(where, grad_branch, weight, qkv, marks, head):
    _, count, cols = qkv.shape
    heads = 2 * cols // (3 * head)
    factor = head ** (-0.5)

    def body(where, grad_branch, weight, qkv, *refs):
        mask = None
        if marks is not None:
            mask = refs[0][...] == refs[1][...]
        out = refs[-1]
        pieces = [[None] * (3 * heads) for _ in range(2)]
        for half in range(2):
            grads = dot_nt(grad_branch[0], weight[2 * half]) + dot_nt(
                grad_branch[1], weight[2 * half + 1]
            )
            grads = grads.astype(LOW)
            for number in range(heads):
                grad = grads[:, number * head : (number + 1) * head]
                query, key, value = head_slices(qkv, half, number, heads, head)
                probs = probabilities(query, key, mask, factor)
                grad_probs = dot_nt(value, grad)
                delta = jnp.sum(grad_probs * probs, axis=0, keepdims=True)
                grad_scores = (probs * (grad_probs - delta)).astype(LOW)
                pieces[half][number] = (dot_tn(key, grad_scores).T * factor).astype(LOW)
                pieces[half][heads + number] = (dot(grad_scores, query) * factor).astype(LOW)
                pieces[half][2 * heads + number] = dot(probs.astype(LOW), grad).astype(LOW)
        per = 3 * heads // 2
        for half in range(2):
            for x in range(2):
                out[2 * half + x] = jnp.concatenate(
                    pieces[half][x * per : (x + 1) * per], axis=1
                )

    ins = [(grad_branch, True), (weight, True), (qkv, True)]
    ins += [] if marks is None else [(m, True) for m in marks]
    return call(
        body,
        where,
        ins,
        [shape(qkv.shape, LOW)],
        [],
        20 * heads * count * count * head,
        "attend_back",
    )[0]


def qkv_back(where, grad_qkv, weight, rows, mods, grad_mid):
    count, features = rows.shape
    cols, many = grad_qkv.shape[-1], len(weight.arrays)

    def body(where, grad_qkv, rows, mods, grad_mid, *refs):
        sources, (out, sums, held, sems) = refs[:many], refs[many:]
        copies = weight.copies(where, sources, held, sems)
        for group in copies:
            start_all(group)
        total = None
        for half in range(2):
            for side in range(2):
                x = lax.rem(where[3] + side, 2)
                wait_all(copies[2 * half + side])
                part = dot_nt(grad_qkv[2 * half + x], held[half, x, :, :cols])
                total = part if total is None else total + part
        normed, inverse = normalize(rows[...].astype(FULL))
        result = grad_mid[...] + normalize_back(total * (1.0 + mods[1:2]), normed, inverse)
        out[...] = result.astype(LOW)
        sums[...] = column_sums(total, total * normed)

    return call(
        body,
        where,
        [(grad_qkv, True), (rows, True), (mods, True), (grad_mid, True)]
        + [(w, False) for w in weight.arrays],
        [shape((count, features), LOW), shape((8, features), FULL)],
        weight.scratch(),
        8 * count * features * cols,
        "qkv_back",
    )


def weight_grad(where, left, right, tail, depth, x_first, half, added):
    blocks, count, wide = left.shape
    blocks = min(blocks, 2)
    rows = blocks * wide // (2 * depth)
    cols = right.shape[-1]
    pairs = [(left, right)]
    if tail is not None:
        pairs.append(tail)
        cols += tail[1].shape[-1] // 2

    def kernel(where, *refs):
        lefts, rights = refs[0 : 2 * len(pairs) : 2], refs[1 : 2 * len(pairs) : 2]
        refs = refs[2 * len(pairs) :]
        far_in, near_in = refs[:2] if added else (None, None)
        refs = refs[2 * (added is not None) :]
        far, near, *flips = refs
        step = pl.program_id(0)

        @pl.when(step == 0)
        def _():
            for source, flipped in zip(lefts, flips):
                size = source.shape[-1]
                for block in range(source.shape[0]):
                    flipped[block * size : (block + 1) * size] = source[block].T

        z = lax.rem(where[0] + step, depth)
        chosen = []
        for flipped in flips:
            size = flipped.shape[0] // depth
            chosen.append(flipped[pl.ds(pl.multiple_of(z * size, 16), size)])

        def product(x):
            value = dot(chosen[0], rights[0][x]).reshape(2, rows, -1)
            if tail is None:
                return [value[0], value[1]]
            more = dot(chosen[1], rights[1][x])
            size, thin = more.shape[0] // 2, more.shape[1] // 2
            found = []
            for y in range(2):
                part = more[y * size : (y + 1) * size]
                strips = jnp.concatenate([part[:, :thin], part[:, thin:]], axis=0)
                found.append(jnp.concatenate([value[y], strips], axis=1))
            return found

        def put(to, place, value, extra):
            if extra is not None:
                value = value + extra[place, 0].astype(FULL)
            to[place, 0] = value.astype(LOW)

        if x_first:
            for to, x, extra in ((far, 1 - where[3], far_in), (near, where[3], near_in)):
                value = product(x)
                for y in range(2):
                    put(to, y, value[y], extra)
        else:
            for x in range(2):
                value = by_place(where[1] == 0, product(x))
                put(near, x, value[0], near_in)
                put(far, x, value[1], far_in)

    def whole(a):
        place = half if a.shape[0] == 4 or (a.shape[0] == 2 and tail is not None and a is tail[0]) else 0
        size = 1 if tail is not None and a is tail[0] else min(a.shape[0], 2)
        return pl.BlockSpec((size,) + a.shape[1:], lambda i, s: (place, 0, 0))

    moving = pl.BlockSpec((2, 1, rows, cols), lambda i, s: (0, i, 0, 0))
    out = shape((2, depth, rows, cols), LOW)
    extra = list(added) if added else []
    operands = [a for pair in pairs for a in pair]
    scratch = [pltpu.VMEM((blocks * wide, count), LOW)]
    if tail is not None:
        scratch.append(pltpu.VMEM((tail[0].shape[-1], count), LOW))
    return pl.pallas_call(
        kernel,
        out_shape=[out, out],
        grid_spec=pltpu.PrefetchScalarGridSpec(
            num_scalar_prefetch=1,
            grid=(depth,),
            in_specs=[whole(a) for a in operands] + [moving] * len(extra),
            out_specs=[moving, moving],
            scratch_shapes=scratch,
        ),
        compiler_params=pltpu.CompilerParams(vmem_limit_bytes=LIMIT),
        cost_estimate=pl.CostEstimate(
            flops=4 * count * blocks * wide * cols,
            bytes_accessed=4 * depth * rows * cols * (4 if added else 2),
            transcendentals=0,
        ),
        name="weight_grad",
    )(where, *operands, *extra)


def add_split(where, near, came, mine):
    _, depth, rows, cols = near.shape

    def kernel(where, near_far, came_far, near_own, came_own, far, own):
        far[...] = (near_far[...].astype(FULL) + came_far[...].astype(FULL)).astype(LOW)
        own[...] = (near_own[...].astype(FULL) + came_own[...].astype(FULL)).astype(LOW)

    def block(other):
        return pl.BlockSpec(
            (pl.squeezed, 1, rows, cols),
            lambda i, s: (1 - s[mine] if other else s[mine], i, 0, 0),
        )

    moving = pl.BlockSpec((1, rows, cols), lambda i, s: (i, 0, 0))
    out = shape((depth, rows, cols), LOW)
    return pl.pallas_call(
        kernel,
        out_shape=[out, out],
        grid_spec=pltpu.PrefetchScalarGridSpec(
            num_scalar_prefetch=1,
            grid=(depth,),
            in_specs=[block(True), block(True), block(False), block(False)],
            out_specs=[moving, moving],
        ),
        compiler_params=pltpu.CompilerParams(vmem_limit_bytes=LIMIT),
        cost_estimate=pl.CostEstimate(
            flops=0, bytes_accessed=12 * depth * rows * cols, transcendentals=0
        ),
        name="add_split",
    )(where, near, came, near, came)


def add_planes(where, near, came):
    depth, rows, cols = near.shape

    def body(where, near, came, own, *others):
        own[...] = near[0].astype(FULL) + came[0].astype(FULL)
        for ahead, out in enumerate(others):
            total = near[ahead + 1].astype(FULL) + came[ahead + 1].astype(FULL)
            out[...] = total.astype(LOW)

    return call(
        body,
        where,
        [(near, True), (came, True)],
        [shape((rows, cols), FULL)] + [shape((rows, cols), LOW)] * (depth - 1),
        [],
        0,
        "add_planes",
    )


def add_last(where, own, came, cols):
    rows, wide = own.shape
    part, thin = rows // 2, wide - cols

    def body(where, own, *refs):
        total = own[...]
        came, outs = refs[: -3 if thin else -2], refs[-3 if thin else -2 :]
        for ref in came:
            total = total + ref[...].astype(FULL)
        first = where[2] == 0
        mine, theirs = by_place(first, [total[:part, :cols], total[part:, :cols]])
        if thin:
            outs[0][...] = jnp.concatenate([total[:part, cols:], total[part:, cols:]], axis=1)
        outs[-2][...] = mine
        outs[-1][...] = theirs.astype(LOW)

    outs = [shape((part, cols), FULL), shape((part, cols), LOW)]
    if thin:
        outs.insert(0, shape((part, 2 * thin), FULL))
    return call(
        body,
        where,
        [(own, True)] + [(c, True) for c in came],
        outs,
        [],
        0,
        "add_last",
    )


def interleave(where, mine, theirs, width):
    rows, cols = mine.shape

    def body(where, mine, theirs, out):
        both = by_place(where[2] == 0, [mine[...], theirs[...].astype(FULL)])
        groups = []
        for at in range(0, cols, width):
            groups += [b[:, at : at + width] for b in both]
        out[...] = jnp.concatenate(groups, axis=1)

    return call(
        body,
        where,
        [(mine, True), (theirs, True)],
        [shape((rows, 2 * cols), FULL)],
        [],
        0,
        "interleave",
    )[0]


def deal(where, shards, widths):
    rows = shards[0].shape[0]
    cols = sum(a.shape[1] for a in shards) // 2

    def body(where, *refs):
        own, other = refs[-2:]
        halves = [[], []]
        for ref, width in zip(refs, widths):
            value = ref[...]
            for number in range(value.shape[1] // width):
                halves[number % 2].append(value[:, number * width : (number + 1) * width])
        pair = [jnp.concatenate(h, axis=1) for h in halves]
        own[...], other[...] = by_place(where[2] == 0, pair)

    return call(
        body,
        where,
        [(a, True) for a in shards],
        [shape((rows, cols), LOW)] * 2,
        [],
        0,
        "deal",
    )


def pack(where, own, got, outs, down, cols):
    part = own.shape[0]
    rows = 2 * part
    thin = outs[0].shape[1] // 2
    wide = down.shape[1]
    padded = -(-wide // 128) * 128
    first = cols[0] + thin

    def body(where, own, got, out_s, out_t, down, qkv_s, up_s, packed):
        pair = by_place(where[2] == 0, [own[...].astype(FULL), got[...].astype(FULL)])
        both = jnp.concatenate(pair, axis=0)

        def strips(ref):
            value = ref[...].astype(FULL)
            return jnp.concatenate([value[:, :thin], value[:, thin:]], axis=0)

        at = cols[0] + cols[1]
        qkv_s[...] = jnp.concatenate([both[:, : cols[0]], strips(out_s)], axis=1).astype(LOW)
        up_s[...] = both[:, cols[0] : at].astype(LOW)
        qkv_t = jnp.concatenate([both[:, at : at + cols[0]], strips(out_t)], axis=1)
        packed[:, :first] = qkv_t.astype(LOW)
        packed[:, first : first + cols[1]] = both[:, at + cols[0] :].astype(LOW)
        for k in range(down.shape[0] // rows):
            lane = first + cols[1] + k * padded
            packed[:, lane : lane + wide] = down[k * rows : (k + 1) * rows]
            if padded > wide:
                packed[:, lane + wide : lane + padded] = jnp.zeros((rows, padded - wide), LOW)

    total = first + cols[1] + down.shape[0] // rows * padded
    return call(
        body,
        where,
        [(a, True) for a in (own, got, *outs, down)],
        [shape((rows, first), LOW), shape((rows, cols[1]), LOW), shape((rows, total), LOW)],
        [],
        0,
        "pack",
    )


def down_grad(where, act, grad_mlp, depth):
    _, count, wide = act.shape
    cols = grad_mlp.shape[-1]
    rows = wide // depth

    def kernel(where, act, grad_mlp, out, flipped):
        step = pl.program_id(0)

        @pl.when(step == 0)
        def _():
            for half in range(2):
                for block in range(2):
                    flipped[half, block * wide : (block + 1) * wide] = act[2 * half + block].T

        for half in range(2):
            core = lax.rem(where[2] + half, 2)
            chosen = flipped[half, at_rows(step, 2 * rows)]
            for x in range(2):
                value = dot(chosen, grad_mlp[x]).astype(LOW)
                for y in range(2):
                    out[0, y, core, x] = value[y * rows : (y + 1) * rows]

    def whole(a):
        return pl.BlockSpec(a.shape, lambda i, s: (0,) * len(a.shape))

    dims = (depth, 2, 2, 2, rows, cols)
    return pl.pallas_call(
        kernel,
        out_shape=shape(dims, LOW),
        grid_spec=pltpu.PrefetchScalarGridSpec(
            num_scalar_prefetch=1,
            grid=(depth,),
            in_specs=[whole(act), whole(grad_mlp)],
            out_specs=pl.BlockSpec((1,) + dims[1:], lambda i, s: (i, 0, 0, 0, 0, 0)),
            scratch_shapes=[pltpu.VMEM((2, 2 * wide, count), LOW)],
        ),
        compiler_params=pltpu.CompilerParams(vmem_limit_bytes=LIMIT),
        cost_estimate=pl.CostEstimate(
            flops=16 * count * wide * cols,
            bytes_accessed=16 * depth * rows * cols,
            transcendentals=0,
        ),
        name="down_grad",
    )(where, act, grad_mlp)


class Grid:
    def __init__(self, patch, seq, patch_axes, seq_axis):
        self.patch_axes, self.seq_axis = patch_axes, seq_axis
        self.every = (patch_axes if isinstance(patch_axes, tuple) else (patch_axes,)) + (seq_axis,)
        self.patch, self.seq = patch, seq
        self.depth = patch // 4
        where = lax.axis_index(patch_axes)
        self.place = where
        self.core = where % 2
        self.y = (where // 2) % 2
        self.z = where // 4
        self.x = lax.axis_index(seq_axis)

    def moves(self, step):
        pairs = []
        for p in range(self.patch):
            for x in range(self.seq):
                z, y, c = p // 4, (p // 2) % 2, p % 2
                z2, y2, c2, x2 = step(z, y, c, x)
                pairs.append((p * self.seq + x, ((z2 * 2 + y2) * 2 + c2) * self.seq + x2))
        return pairs

    def send(self, array, step):
        return lax.ppermute(array, self.every, self.moves(step))

    def flip_core(self, array):
        return self.send(array, lambda z, y, c, x: (z, y, 1 - c, x))

    def flip_y(self, array):
        return self.send(array, lambda z, y, c, x: (z, 1 - y, c, x))

    def shift_x(self, array, by):
        return self.send(array, lambda z, y, c, x: (z, y, c, (x + by) % self.seq))

    def shift_z(self, array, by):
        return self.send(array, lambda z, y, c, x: ((z + by) % self.depth, y, c, x))

    def xor_patch(self, array, bit):
        pairs = [
            (p * self.seq + x, (p ^ bit) * self.seq + x)
            for p in range(self.patch)
            for x in range(self.seq)
        ]
        return lax.ppermute(array, self.every, pairs)

    def bits(self):
        bit = self.patch // 2
        while bit:
            yield bit
            bit //= 2

    def sum_patch(self, array):
        for bit in self.bits():
            array = array + self.xor_patch(array, bit)
        return array

    def join_patch(self, array, bit):
        other = self.xor_patch(array, bit)
        mine_first = (self.place // bit) % 2 == 0
        return jnp.where(
            mine_first, jnp.concatenate([array, other]), jnp.concatenate([other, array])
        )

    def all_seq(self, array):
        return [array] + [self.shift_x(array, -j) for j in range(1, self.seq)]


class Split:
    def __init__(self, grid, head, group):
        self.grid = grid
        self.head, self.group = head, group
        self.last = None
        self.where = jnp.stack([grid.z, grid.y, grid.core, grid.x]).astype(jnp.int32)

    @staticmethod
    def fits(patch, seq, frames, features, hidden):
        return (
            patch == HEADS
            and patch == frames
            and seq == 2
            and features % (2 * patch) == 0
            and hidden % patch == 0
            and (2 * features // patch) % 16 == 0
            and hidden == 2 * 2 * features
            and (hidden // patch) % 32 == 0
        )


    def tie(self, *arrays):
        if self.last is not None:
            *arrays, self.last = lax.optimization_barrier((*arrays, self.last))
        return arrays[0] if len(arrays) == 1 else arrays

    def done(self, array):
        self.last = array
        return array

    def run(self, kernel, first, *rest):
        result = kernel(self.where, self.tie(first), *rest)
        self.last = result[-1] if isinstance(result, (list, tuple)) else result
        return result

    def first(self, array, x_first):
        return self.grid.shift_x(array, 1) if x_first else self.grid.flip_y(array)

    def prepare(self, spatial, temporal):
        own, other = deal(
            self.where,
            [spatial[0], spatial[2], temporal[0], temporal[2]],
            [self.head, self.group] * 2,
        )
        got = self.grid.flip_core(other)
        cols = (spatial[0].shape[1] // 2, spatial[2].shape[1] // 2)
        return pack(self.where, own, got, [spatial[1], temporal[1]], temporal[3], cols)

    def gather(self, piece, by_rows):
        grid = self.grid
        rows, cols = piece.shape
        cut = rows // 2 if by_rows else (cols // 256 + 1) * 128
        piece = self.tie(piece)
        pieces = [piece] + [grid.shift_z(piece, -j) for j in range(1, grid.depth)]
        yield
        if by_rows:
            strips = [[p[:cut] for p in pieces], [p[cut:] for p in pieces]]
            places = [(0, cut, 0, cols), (cut, rows - cut, 0, cols)]
        else:
            strips = [[p[:, :cut] for p in pieces], [p[:, cut:] for p in pieces]]
            places = [(0, rows, 0, cut), (0, rows, cut, cols - cut)]
        held = self.tie(*[jnp.stack(s) for s in strips])
        self.done(held[1])
        came = [self.first(h, order) for h, order in zip(held, (True, False))]
        yield
        held = self.tie(*[jnp.stack([h, c]) for h, c in zip(held, came)])
        self.done(held[1])
        came = [self.first(h, order) for h, order in zip(held, (False, True))]
        found = []
        for h, c, order, place in zip(held, came, (True, False), places):
            arrays = [h, c, grid.flip_core(h), grid.flip_core(c)]
            found.append((arrays, order, 0) + place)
        yield Weight(grid.depth, rows, cols, found)

    def gather_packed(self, packed, cols, down):
        grid = self.grid
        rows, lanes = packed.shape
        whole = lax.all_gather(self.tie(packed), grid.every, axis=0)
        arrays = [whole.reshape(grid.depth, 2, 2, 2, rows, lanes)]
        at, found = 0, []
        for c in cols:
            found.append(Weight(grid.depth, rows, c, [(arrays, None, at, 0, rows, 0, c)]))
            at += c
        count = down[0] // rows
        padded = (lanes - at) // count
        strips = [
            (arrays, None, at + k * padded, k * rows, rows, 0, padded) for k in range(count)
        ]
        found.append(Weight(grid.depth, down[0], down[1], strips))
        return found

    def reduce(self, left, right, tail, x_first, width):
        grid = self.grid
        depth = grid.depth
        cols = right.shape[-1]
        far, near = self.run(weight_grad, left, right, tail, depth, x_first, 1, None)
        came = grid.flip_core(far), grid.flip_core(near)
        yield
        far, near = self.run(weight_grad, left, right, tail, depth, x_first, 0, came)
        came = self.first(far, x_first)
        yield
        far, near = self.run(add_split, near, came, 1 if x_first else 3)
        came = self.first(far, not x_first)
        yield
        own, *others = self.run(add_planes, near, came)
        came = [grid.shift_z(plane, j + 1) for j, plane in enumerate(others)]
        yield
        *rest, mine, theirs = self.run(add_last, own, came, cols)
        theirs = grid.flip_core(theirs)
        yield
        whole = self.run(interleave, mine, theirs, width)
        yield [whole] + rest

    def scatter(self, grads):
        dims = grads.shape[-2:]
        mine = lax.psum_scatter(
            grads.reshape((-1,) + dims), self.grid.every, scatter_dimension=0, tiled=False
        )
        return mine.reshape(dims).astype(FULL)

    def qkv_part(self, rows, mods, weight, marks):
        cols = 3 * rows.shape[1] // 4
        hidden_one, out_w, qkv = self.run(norm_qkv, rows, mods, weight, cols)
        attended = self.run(attend_kernel, qkv, marks, self.head)
        branch, middle, hidden_two = self.run(out_norm, rows, mods, attended, out_w)
        return rows, hidden_one, out_w, qkv, attended, branch, middle, hidden_two

    def forward(self, tokens, mods, shards, marks, to_patches):
        (qkv_s, up_s, down_s), packed = shards
        cols = (qkv_s.shape[1], up_s.shape[1])
        qkv_g = self.gather(qkv_s, False)
        next(qkv_g)
        next(qkv_g)
        up_g = self.gather(up_s, False)
        next(up_g)
        next(up_g)
        qkv_w = next(qkv_g)
        down_g = self.gather(down_s, True)
        next(down_g)
        next(down_g)
        up_w = next(up_g)
        temporal = self.gather_packed(packed, cols, down_s.shape)
        saved = self.qkv_part(tokens, mods[0], qkv_w, None)
        down_w = next(down_g)
        pre, act = self.run(up_gelu, saved[-1], up_w)
        mlp, result = self.run(down_add, act, down_w, saved[-2], mods[0])
        spatial = (mods[0], (qkv_w, up_w, down_w), saved + (pre, act, mlp), None)

        saved = self.qkv_part(to_patches(result), mods[1], temporal[0], marks)
        pre, act = self.run(up_gelu, saved[-1], temporal[1])
        mlp, result = self.run(down_add, act, temporal[2], saved[-2], mods[1])
        return result, spatial, (mods[1], temporal, saved + (pre, act, mlp), marks)

    def backward(self, spatial, temporal, grad, move, condition_steps):
        depth, head = self.grid.depth, self.head
        mods, (qkv_w, up_w, down_w), saved, marks = temporal
        rows, hidden_one, out_w, qkv, attended, branch, middle, hidden_two, pre, act, mlp = saved
        grad_mlp = self.run(scale_halves, grad, mods)
        down_t = self.scatter(self.run(down_grad, act, grad_mlp, depth))
        grad_mid, grad_pre, grad_branch, sums_two = self.run(
            mlp_back, grad, mods, pre, middle, branch, mlp, up_w, down_w
        )
        up_t = self.reduce(hidden_two[None], grad_pre, None, True, self.group)
        next(up_t)
        grad_rows = self.run(attend_back_kernel, grad_branch, out_w, qkv, marks, head)
        next(up_t)
        qkv_t = self.reduce(hidden_one[None], grad_rows, (attended, grad_branch), False, head)
        next(qkv_t)
        grad, sums_one = self.run(qkv_back, grad_rows, qkv_w, rows, mods, grad_mid)
        mods_t = jnp.concatenate([sums_one[:2], sums_two[:4]], axis=0).reshape(1, -1)
        grad = move(grad)
        next(qkv_t)

        mods, (qkv_w, up_w, down_w), saved, marks = spatial
        rows, hidden_one, out_w, qkv, attended, branch, middle, hidden_two, pre, act, mlp = saved
        grad_mlp = self.run(scale_halves, grad, mods)
        down_s = self.scatter(self.run(down_grad, act, grad_mlp, depth))
        next(up_t)
        grad_mid, grad_pre, grad_branch, sums_two = self.run(
            mlp_back, grad, mods, pre, middle, branch, mlp, up_w, down_w
        )
        up_s = self.reduce(hidden_two[None], grad_pre, None, True, self.group)
        next(up_s)
        next(qkv_t)
        grad_rows = self.run(attend_back_kernel, grad_branch, out_w, qkv, marks, head)
        next(up_s)
        next(up_t)
        qkv_s = self.reduce(hidden_one[None], grad_rows, (attended, grad_branch), False, head)
        next(qkv_s)
        next(qkv_t)
        grad, sums_one = self.run(qkv_back, grad_rows, qkv_w, rows, mods, grad_mid)
        mods_s = jnp.concatenate([sums_one[:2], sums_two[:4]], axis=0).reshape(1, -1)
        next(qkv_s)
        next(up_t)
        steps = condition_steps(mods_s, mods_t)
        for _ in range(2):
            next(steps)
        next(up_s)
        for _ in range(3):
            next(steps)
        next(qkv_t)
        next(qkv_s)
        (up_t,) = next(up_t)
        next(up_s)
        qkv_t, out_t = next(qkv_t)
        for _ in range(3):
            next(steps)
        next(qkv_s)
        next(up_s)
        conditions = list(steps)[-1]
        (up_s,) = next(up_s)
        next(qkv_s)
        qkv_s, out_s = next(qkv_s)
        return grad, conditions, (qkv_s, out_s, up_s, down_s), (qkv_t, out_t, up_t, down_t)


class WholeWeights:
    def __init__(self, grid, features, hidden):
        self.features, self.hidden = features, hidden

    def gather(self, local):
        wide = lax.all_gather(local, "seq", axis=1, tiled=True)
        return lax.all_gather(wide, "patch", axis=0, tiled=True)

    def fetch(self, spatial, temporal):
        return [[tuple(self.gather(w) for w in block)] for block in (spatial, temporal)]

    def scatter(self, grad):
        rows = lax.psum_scatter(grad.astype(LOW), "patch", scatter_dimension=0, tiled=True)
        return lax.psum_scatter(rows, "seq", scatter_dimension=1, tiled=True).astype(FULL)

    def reduce_mlp(self, hidden, grad_pre, activated, grad_mlp, flip):
        return (
            self.scatter(matmul_tn(hidden, grad_pre[0])),
            self.scatter(matmul_tn(activated[0], grad_mlp)),
        )

    def reduce_out(self, attended, grad_branch, flip):
        return self.scatter(matmul_tn(attended[0], grad_branch))

    def reduce_qkv(self, hidden, grad_qkv, flip):
        return self.scatter(matmul_tn(hidden, grad_qkv[0]))


def attention(queries, keys, mask, factor):
    scores = jnp.einsum("bphd,bkhd->bhpk", queries, keys, preferred_element_type=FULL) * factor
    if mask is not None:
        scores = jnp.where(mask, scores, -1e30)
    top = jnp.max(scores, axis=-1, keepdims=True)
    weights = jnp.exp(scores - top)
    return weights / jnp.sum(weights, axis=-1, keepdims=True)


def attend(qkv, batch, mask, head, share):
    rows = qkv.reshape(batch, -1, 3, qkv.shape[-1] // (3 * head), head)
    keys, values = share(rows[:, :, 1]), share(rows[:, :, 2])
    probs = attention(rows[:, :, 0], keys, mask, head ** (-0.5)).astype(LOW)
    mixed = jnp.einsum("bhpk,bkhd->bphd", probs, values, preferred_element_type=FULL)
    return mixed.reshape(qkv.shape[0], -1).astype(LOW)


def attend_back(grad, qkv, batch, mask, head, share, share_back):
    factor = head ** (-0.5)
    heads = qkv.shape[-1] // (3 * head)
    rows = qkv.reshape(batch, -1, 3, heads, head)
    grad_rows = grad.reshape(batch, -1, heads, head)
    queries, keys, values = rows[:, :, 0], share(rows[:, :, 1]), share(rows[:, :, 2])
    probs = attention(queries, keys, mask, factor)
    grad_probs = jnp.einsum("bphd,bkhd->bhpk", grad_rows, values, preferred_element_type=FULL)
    delta = jnp.sum(grad_probs * probs, axis=-1, keepdims=True)
    grad_scores = (probs * (grad_probs - delta)).astype(LOW)
    grad_queries = (
        jnp.einsum("bhpk,bkhd->bphd", grad_scores, keys, preferred_element_type=FULL) * factor
    )
    grad_keys = (
        jnp.einsum("bhpk,bphd->bkhd", grad_scores, queries, preferred_element_type=FULL) * factor
    )
    grad_values = jnp.einsum(
        "bhpk,bphd->bkhd", probs.astype(LOW), grad_rows, preferred_element_type=FULL
    )
    joined = jnp.stack(
        [grad_queries, share_back(grad_keys), share_back(grad_values)], axis=2
    )
    return joined.reshape(qkv.shape[0], -1).astype(LOW)


def total_parts(parts):
    total = parts[0]
    for part in parts[1:]:
        total = total + part
    return total


def block_forward(residual, pieces, parts, mix):
    normed_one, inverse_one = normalize(residual)
    hidden_one = (normed_one * (1.0 + pieces[1]) + pieces[0]).astype(LOW)
    qkv = [matmul(hidden_one, part[0]).astype(LOW) for part in parts]
    attended = [mix(rows) for rows in qkv]
    branch = total_parts([matmul(a, part[1]) for a, part in zip(attended, parts)])
    middle = residual + pieces[2] * branch
    normed_two, inverse_two = normalize(middle)
    hidden_two = (normed_two * (1.0 + pieces[4]) + pieces[3]).astype(LOW)
    pre = [matmul(hidden_two, part[2]) for part in parts]
    activated = [jax.nn.gelu(v, approximate=True).astype(LOW) for v in pre]
    mlp = total_parts([matmul(a, part[3]) for a, part in zip(activated, parts)])
    result = middle + pieces[5] * mlp
    saved = (
        normed_one,
        inverse_one,
        hidden_one,
        qkv,
        attended,
        branch,
        normed_two,
        inverse_two,
        hidden_two,
        pre,
        activated,
        mlp,
    )
    return result, saved


def block_backward(incoming, pieces, parts, saved, mix_back, weights, groups, flip):
    (
        normed_one,
        inverse_one,
        hidden_one,
        qkv,
        attended,
        branch,
        normed_two,
        inverse_two,
        hidden_two,
        pre,
        activated,
        mlp,
    ) = saved
    grad_mlp = (pieces[5] * incoming).astype(LOW)
    grad_pre = []
    for part, v in zip(parts, pre):
        _, back = jax.vjp(partial(jax.nn.gelu, approximate=True), v)
        grad_pre.append(back(matmul_nt(grad_mlp, part[3]))[0].astype(LOW))
    grad_up, grad_down = weights.reduce_mlp(hidden_two, grad_pre, activated, grad_mlp, flip)
    grad_hidden_two = total_parts([matmul_nt(g, part[2]) for g, part in zip(grad_pre, parts)])
    grad_middle = incoming + normalize_back(
        grad_hidden_two * (1.0 + pieces[4]), normed_two, inverse_two
    )
    grad_branch = (pieces[2] * grad_middle).astype(LOW)
    grad_out = weights.reduce_out(attended, grad_branch, flip)
    grad_attended = [matmul_nt(grad_branch, part[1]).astype(LOW) for part in parts]
    grad_qkv_rows = [mix_back(g, rows) for g, rows in zip(grad_attended, qkv)]
    grad_qkv = weights.reduce_qkv(hidden_one, grad_qkv_rows, flip)
    grad_hidden_one = total_parts(
        [matmul_nt(g, part[0]) for g, part in zip(grad_qkv_rows, parts)]
    )
    grad_residual = grad_middle + normalize_back(
        grad_hidden_one * (1.0 + pieces[1]), normed_one, inverse_one
    )
    sums = [
        jnp.sum(v.reshape(groups, -1, v.shape[-1]), axis=1)
        for v in (
            grad_hidden_one,
            grad_hidden_one * normed_one,
            grad_middle * branch,
            grad_hidden_two,
            grad_hidden_two * normed_two,
            incoming * mlp,
        )
    ]
    grad_mods = jnp.concatenate(sums, axis=-1)
    return grad_residual, grad_mods, (grad_qkv, grad_out, grad_up, grad_down)


def per_device(
    patch,
    seq,
    patch_axes,
    seq_axis,
    tokens,
    cotangent,
    class_ids,
    timesteps,
    segments,
    class_table,
    mod_spatial,
    qkv_spatial,
    out_spatial,
    up_spatial,
    down_spatial,
    mod_temporal,
    qkv_temporal,
    out_temporal,
    up_temporal,
    down_temporal,
):
    groups, frames, patch_rows, features = tokens.shape
    row_count = groups * frames * patch_rows
    head = features // HEADS
    hidden = up_spatial.shape[1] * seq
    grid = Grid(patch, seq, patch_axes, seq_axis)
    split = groups == 1 and Split.fits(patch, seq, frames, features, hidden)

    ways = max(1, patch // frames)
    subgroups = None
    if ways > 1:
        subgroups = [[a * ways + b for a in range(frames)] for b in range(ways)]

    def to_frames(array):
        moved = lax.all_to_all(
            array.reshape(groups, frames, patch_rows, features),
            patch_axes,
            split_axis=1,
            concat_axis=2,
            tiled=True,
            axis_index_groups=subgroups,
        )
        return moved.reshape(row_count, features)

    own_frames = max(1, frames // patch)

    def to_patches(array):
        moved = lax.all_to_all(
            array.reshape(groups, own_frames, -1, features),
            patch_axes,
            split_axis=2,
            concat_axis=1,
            tiled=True,
            axis_index_groups=subgroups,
        )
        return moved.reshape(row_count, features)

    def sharers(by):
        return [
            (a * ways + b, a * ways + (b + by) % ways)
            for a in range(patch // ways)
            for b in range(ways)
        ]

    def share_frame(array):
        if ways == 1:
            return array
        return jnp.concatenate(
            [array] + [lax.ppermute(array, patch_axes, sharers(j)) for j in range(1, ways)], axis=1
        )

    def share_frame_back(array):
        if ways == 1:
            return array
        cut = jnp.split(array, ways, axis=1)
        total = cut[0]
        for j in range(1, ways):
            total = total + lax.ppermute(cut[j], patch_axes, sharers(-j))
        return total

    one_hot = (
        class_ids[:, None] == jnp.arange(class_table.shape[0], dtype=jnp.int32)[None, :]
    ).astype(LOW)
    condition = matmul(one_hot, class_table) + time_features(timesteps, features)
    conditions = grid.all_seq(condition)
    every_class = grid.all_seq(class_ids)
    cond_low = [jax.nn.silu(c).astype(LOW) for c in conditions]
    mod_rows = features // patch
    first_row = grid.place * mod_rows
    cond_own = [lax.dynamic_slice_in_dim(c, first_row, mod_rows, axis=1) for c in cond_low]
    partial_mods = [
        jnp.stack([matmul(c, mod_spatial), matmul(c, mod_temporal)]) for c in cond_own
    ]
    mods = grid.sum_patch(jnp.stack(partial_mods))
    received = [mods[0]] + [grid.shift_x(mods[j], j) for j in range(1, seq)]
    ordered = in_order(received[:1] + received[:0:-1], grid.x)
    modulation = jnp.concatenate(ordered, axis=-1)

    width = mod_spatial.shape[1]

    def outer(columns):
        return lax.dot_general(
            jnp.concatenate(cond_own).astype(FULL),
            columns,
            (((0,), (0,)), ((), ())),
            precision=PRECISE,
            preferred_element_type=FULL,
        )

    def condition_part(columns, mod):
        return lax.dot_general(
            columns,
            mod.astype(FULL),
            (((1,), (1,)), ((), ())),
            precision=PRECISE,
            preferred_element_type=FULL,
        )

    def condition_steps(spatial_sums, temporal_sums, hold):
        sums = jnp.stack([spatial_sums, temporal_sums])
        for bit in grid.bits():
            sums = hold(sums + grid.xor_patch(sums, bit))
            yield None
        sums = sums.reshape(2, groups, seq, width)
        columns = [pick(sums, 2, grid.x)] + [
            grid.shift_x(pick(sums, 2, (grid.x - j) % seq), -j) for j in range(1, seq)
        ]
        columns = hold(jnp.concatenate(columns, axis=1))
        yield None
        parts = condition_part(columns[0], mod_spatial) + condition_part(columns[1], mod_temporal)
        parts = parts.reshape(seq, groups, mod_rows)
        total = parts
        for j in range(1, seq):
            total = total + jnp.roll(grid.shift_x(parts, j), j, axis=0)
        total = hold(total[None])
        yield None
        bit = 1
        while bit < patch:
            total = hold(grid.join_patch(total, bit))
            bit *= 2
            yield None
        grad_condition = total.transpose(1, 2, 0, 3).reshape(seq * groups, features)
        _, silu_back = jax.vjp(jax.nn.silu, jnp.concatenate(conditions))
        every_hot = (
            jnp.concatenate(every_class)[:, None]
            == jnp.arange(class_table.shape[0], dtype=jnp.int32)[None, :]
        ).astype(FULL)
        grad_class_table = lax.dot_general(
            every_hot,
            silu_back(grad_condition)[0],
            (((0,), (0,)), ((), ())),
            precision=PRECISE,
            preferred_element_type=FULL,
        )
        yield grad_class_table, outer(columns[0]), outer(columns[1])


    spatial_shards = (qkv_spatial, out_spatial, up_spatial, down_spatial)
    temporal_shards = (qkv_temporal, out_temporal, up_temporal, down_temporal)
    span = frames * patch_rows
    patch_of = jnp.arange(span, dtype=jnp.int32) % patch_rows
    place_of = jnp.repeat(segments, patch_rows, axis=1) * patch_rows + patch_of[None, :]

    if split:
        plan = Split(grid, head, hidden // patch)
        mods_of = [
            jnp.pad(modulation[block].reshape(6, features), ((0, 2), (0, 0))) for block in range(2)
        ]
        marks = (place_of.reshape(-1, 1), place_of.reshape(1, -1))
        qkv_s, up_s, packed = plan.prepare(spatial_shards, temporal_shards)
        frame_tokens = to_frames(tokens)
        plan.done(mods_of[0])
        frame_tokens = plan.done(plan.tie(frame_tokens))
        result, spatial_state, temporal_state = plan.forward(
            frame_tokens,
            mods_of,
            ((qkv_s, up_s, down_spatial), packed),
            marks,
            to_patches,
        )
        out_tokens = result.reshape(tokens.shape)
        grad_spatial_in, condition_grads, spatial_grads, temporal_grads = plan.backward(
            spatial_state,
            temporal_state,
            cotangent.reshape(row_count, features),
            to_frames,
            lambda s, t: condition_steps(s, t, lambda v: plan.done(plan.tie(v))),
        )
        grad_tokens = to_patches(grad_spatial_in).astype(FULL).reshape(tokens.shape)
    else:
        weights = WholeWeights(grid, features, hidden)

        def pieces_of(block):
            rows = modulation[block]
            if groups > 1:
                rows = jnp.repeat(rows, row_count // groups, axis=0)
            return [rows[:, k * features : (k + 1) * features] for k in range(6)]

        spatial_pieces, temporal_pieces = pieces_of(0), pieces_of(1)
        spatial_parts, temporal_parts = weights.fetch(spatial_shards, temporal_shards)
        same = (place_of[:, :, None] == place_of[:, None, :])[:, None, :, :]
        itself = lambda array: array
        spatial_batch = groups * own_frames
        spatial_mix = lambda rows: attend(rows, spatial_batch, None, head, share_frame)
        spatial_mix_back = lambda g, rows: attend_back(
            g, rows, spatial_batch, None, head, share_frame, share_frame_back
        )
        temporal_mix = lambda rows: attend(rows, groups, same, head, itself)
        temporal_mix_back = lambda g, rows: attend_back(
            g, rows, groups, same, head, itself, itself
        )
        spatial_in = to_frames(tokens).astype(FULL)
        spatial_out, spatial_saved = block_forward(
            spatial_in, spatial_pieces, spatial_parts, spatial_mix
        )
        temporal_in = to_patches(spatial_out.astype(LOW)).astype(FULL)
        result, temporal_saved = block_forward(
            temporal_in, temporal_pieces, temporal_parts, temporal_mix
        )
        out_tokens = result.astype(LOW).reshape(tokens.shape)
        incoming = cotangent.astype(FULL).reshape(row_count, features)
        grad_temporal_in, temporal_sums, temporal_grads = block_backward(
            incoming,
            temporal_pieces,
            temporal_parts,
            temporal_saved,
            temporal_mix_back,
            weights,
            groups,
            True,
        )
        grad_spatial_out = to_frames(grad_temporal_in.astype(LOW)).astype(FULL)
        grad_spatial_in, spatial_sums, spatial_grads = block_backward(
            grad_spatial_out,
            spatial_pieces,
            spatial_parts,
            spatial_saved,
            spatial_mix_back,
            weights,
            groups,
            False,
        )
        grad_tokens = to_patches(grad_spatial_in.astype(LOW)).astype(FULL).reshape(tokens.shape)
        condition_grads = list(condition_steps(spatial_sums, temporal_sums, itself))[-1]

    grad_class_table, grad_mod_spatial, grad_mod_temporal = condition_grads

    return (
        out_tokens,
        grad_tokens,
        grad_class_table,
        grad_mod_spatial,
        *spatial_grads,
        grad_mod_temporal,
        *temporal_grads,
    )


def solution(mesh):
    patch, seq = mesh.shape["patch"], mesh.shape["seq"]
    patch_axes, seq_axis = "patch", "seq"
    if seq == 2 and patch % 4 == 0:
        patch_axes, seq_axis = ("z", "y", "core"), "x"
        mesh = Mesh(mesh.devices.reshape(patch // 4, 2, 2, seq), patch_axes + (seq_axis,))
    rows = P(seq_axis, None, patch_axes, None)
    both = P(patch_axes, seq_axis)
    return jax.shard_map(
        partial(per_device, patch, seq, patch_axes, seq_axis),
        mesh=mesh,
        in_specs=(rows, rows, P(seq_axis), P(seq_axis), P(seq_axis, None), P()) + (both,) * 10,
        out_specs=(rows, rows, P()) + (both,) * 10,
        check_vma=False,
    )
```

```python
import math
from functools import partial

import jax
import jax.numpy as jnp
from jax import lax
from jax.experimental import pallas as pl
from jax.experimental.pallas import tpu as pltpu
from jax.sharding import Mesh
from jax.sharding import PartitionSpec as P

HEADS = 16
EPSILON = 1e-06
PRECISE = lax.Precision.HIGHEST
LOW = jnp.bfloat16
FULL = jnp.float32


def time_features(step_ids, features):
    half_width = features // 2
    frequency = jnp.exp(-math.log(10000.0) * jnp.arange(half_width, dtype=FULL) / half_width)
    angles = step_ids.astype(FULL)[:, None] * frequency[None, :]
    return jnp.concatenate([jnp.cos(angles), jnp.sin(angles)], axis=-1)


def normalize(values):
    centred = values - jnp.mean(values, axis=-1, keepdims=True)
    inverse = lax.rsqrt(jnp.mean(centred * centred, axis=-1, keepdims=True) + EPSILON)
    return centred * inverse, inverse


def normalize_back(grad_norm, normed, inverse):
    return inverse * (
        grad_norm
        - jnp.mean(grad_norm, axis=-1, keepdims=True)
        - normed * jnp.mean(grad_norm * normed, axis=-1, keepdims=True)
    )


def matmul(left, right):
    return jnp.dot(left, right, preferred_element_type=FULL)


def matmul_nt(left, right):
    return lax.dot_general(left, right, (((1,), (1,)), ((), ())), preferred_element_type=FULL)


def matmul_tn(left, right):
    return lax.dot_general(left, right, (((0,), (0,)), ((), ())), preferred_element_type=FULL)


def in_order(pieces, first):
    count = len(pieces)
    return [lax.select_n((k - first) % count, *pieces) for k in range(count)]


def pick(array, axis, index):
    return lax.dynamic_index_in_dim(array, index, axis, keepdims=False)


LIMIT = 60 * 2**20
TINY = pl.CostEstimate(flops=1, bytes_accessed=1, transcendentals=0)
CHIPS_Y = 2


def at_rows(index, rows):
    return pl.ds(pl.multiple_of(index * rows, 16), rows)


class Weight:
    def __init__(self, depth, rows, cols, strips):
        self.depth, self.rows, self.cols, self.strips = depth, rows, cols, strips
        self.width = max(strip[6] + strip[7] for strip in strips)
        self.arrays = []
        for strip in strips:
            if not any(strip[0][0] is array for array in self.arrays):
                self.arrays += strip[0]

    def scratch(self):
        return [
            pltpu.VMEM((2, 2 * self.depth * self.rows, self.width), LOW),
            pltpu.SemaphoreType.DMA((2, 2, self.depth * len(self.strips))),
        ]

    def copies(self, where, refs, held, sems):
        found = []
        for side in range(2):
            group = []
            x = lax.rem(where[3] + side, 2)
            for turn in range(2):
                y = lax.rem(where[1] + turn, 2)
                for ahead in range(self.depth):
                    z = lax.rem(where[0] + ahead, self.depth)
                    at = (z * CHIPS_Y + y) * self.rows
                    for number, strip in enumerate(self.strips):
                        arrays, x_first, z_placed, source_lane, row, rows, lane, lanes = strip
                        base = [k for k, a in enumerate(self.arrays) if a is arrays[0]][0]
                        first, second = (side, turn) if x_first else (turn, side)
                        source = refs[base + second].at[
                            first,
                            z if z_placed else ahead,
                            :,
                            source_lane : source_lane + lanes,
                        ]
                        start = pl.multiple_of(at + row, 16)
                        target = held.at[x, pl.ds(start, rows), lane : lane + lanes]
                        sem = sems.at[side, turn, ahead * len(self.strips) + number]
                        group.append(pltpu.make_async_copy(source, target, sem))
            found.append(group)
        return found


def start_all(copies):
    for copy in copies:
        copy.start()


def wait_all(copies):
    for copy in copies:
        copy.wait()


def dot(left, right):
    return lax.dot_general(left, right, (((1,), (0,)), ((), ())), preferred_element_type=FULL)


def dot_nt(left, right):
    return lax.dot_general(left, right, (((1,), (1,)), ((), ())), preferred_element_type=FULL)


def dot_tn(left, right):
    return lax.dot_general(left, right, (((0,), (0,)), ((), ())), preferred_element_type=FULL)


def call(body, where, ins, outs, scratch, flops, name, after=()):
    count = len(ins)

    def kernel(where_ref, *refs):
        body(where_ref, *refs[:count], *refs[count + len(after) :])

    vmem = pl.BlockSpec(memory_space=pltpu.VMEM)
    hbm = pl.BlockSpec(memory_space=pl.ANY)
    size = sum(a.size * a.dtype.itemsize for a, _ in ins)
    size += sum(math.prod(o.shape) * o.dtype.itemsize for o in outs)
    return pl.pallas_call(
        kernel,
        out_shape=outs,
        in_specs=[pl.BlockSpec(memory_space=pltpu.SMEM)]
        + [vmem if inside else hbm for _, inside in ins]
        + [hbm] * len(after),
        out_specs=[vmem] * len(outs),
        scratch_shapes=scratch,
        compiler_params=pltpu.CompilerParams(vmem_limit_bytes=LIMIT),
        cost_estimate=TINY,
        name=name,
    )(where, *[a for a, _ in ins], *after)


def shape(dims, dtype):
    return jax.ShapeDtypeStruct(dims, dtype)


def by_place(first, pair):
    return [jnp.where(first, pair[0], pair[1]), jnp.where(first, pair[1], pair[0])]


def two_cores(refs):
    return jnp.concatenate([ref[...].astype(FULL) for ref in refs], axis=0)


def add_core(part, came):
    count = part.shape[0] // 2
    part, came = part[...].astype(FULL), came[...].astype(FULL)
    return jnp.concatenate([part[:count] + came[count:], part[count:] + came[:count]], axis=0)


def norm_qkv(where, rows, mods, weight, cols):
    count, features = rows[0].shape
    count *= 2
    many = len(weight.arrays)
    thin = weight.cols - cols
    chips = 2 * weight.depth
    part = weight.rows // 2

    def body(where, own, other, mods, *refs):
        sources, (hidden, out_weight, out, held, sems) = refs[:many], refs[many:]
        copies = weight.copies(where, sources, held, sems)
        for group in copies:
            start_all(group)
        normed, _ = normalize(two_cores((own, other)))
        value = (normed * (1.0 + mods[1:2]) + mods[0:1]).astype(LOW)
        hidden[0] = value
        for side in range(2):
            x = lax.rem(where[3] + side, 2)
            wait_all(copies[side])
            out[x] = dot(value, held[x, :, :cols]).astype(LOW)
            strips = held[x, :, cols:].astype(FULL).reshape(chips, 2, part, thin)
            both = [strips[:, k].reshape(chips * part, thin) for k in range(2)]
            out_weight[x] = jnp.concatenate(both, axis=1).astype(LOW)

    return call(
        body,
        where,
        [(a, True) for a in (*rows, mods)] + [(w, False) for w in weight.arrays],
        [
            shape((1, count, features), LOW),
            shape((2, chips * part, 2 * thin), LOW),
            shape((2, count, cols), LOW),
        ],
        weight.scratch(),
        4 * count * features * cols,
        "norm_qkv",
    )


def head_slices(qkv, rows, number, heads, head):
    def column(slot):
        per = 3 * heads // 2
        x, at = divmod(slot, per)
        return qkv[x, rows, at * head : (at + 1) * head]

    return column(number), column(heads + number), column(2 * heads + number)


def probabilities(query, key, mask, factor):
    scores = dot_nt(key, query) * factor
    if mask is not None:
        scores = jnp.where(mask, scores, -1e30)
    weights = jnp.exp(scores - jnp.max(scores, axis=0, keepdims=True))
    return weights * (1.0 / jnp.sum(weights, axis=0, keepdims=True))


def attend_out(where, qkv, out_weight, marks, head):
    _, count, cols = qkv.shape
    heads = 2 * cols // (3 * head)
    size = count // 2

    def body(where, qkv, out_weight, *refs):
        mask = None
        if marks is not None:
            mask = refs[0][...] == refs[1][...]
        attended, part = refs[-2:]
        for block in range(2):
            rows = slice(block * size, (block + 1) * size)
            mixed = []
            for number in range(heads):
                query, key, value = head_slices(qkv, rows, number, heads, head)
                probs = probabilities(query, key, mask, head ** (-0.5)).astype(LOW)
                mixed.append(dot_tn(value, probs))
            result = jnp.concatenate(mixed, axis=0).T.astype(LOW)
            attended[0, rows] = result
            sides = [dot(result, out_weight[x]) for x in range(2)]
            part[rows] = jnp.concatenate(sides, axis=1).astype(LOW)

    ins = [(qkv, True), (out_weight, True)] + ([] if marks is None else [(m, True) for m in marks])
    return call(
        body,
        where,
        ins,
        [shape((1, count, heads * head), LOW), shape((count, 2 * out_weight.shape[2]), LOW)],
        [],
        8 * heads * count * size * head,
        "attend_out",
    )


GELU_A = math.sqrt(2.0 / math.pi)
GELU_B = 0.044715


def gelu(value):
    inner = GELU_A * (value + GELU_B * value * value * value)
    return 0.5 * value * (1.0 + jnp.tanh(inner))


def gelu_slope(value):
    square = value * value
    bend = jnp.tanh(GELU_A * (value + GELU_B * square * value))
    return 0.5 * (1.0 + bend) + 0.5 * value * (1.0 - bend * bend) * GELU_A * (
        1.0 + 3.0 * GELU_B * square
    )


def norm_up(where, part, came, rows, mods, weight):
    count, features = part.shape
    cols, many = weight.cols, len(weight.arrays)

    def body(where, part, came, own, other, mods, *refs):
        sources, (branch, middle, hidden, pre, act, held, sems) = refs[:many], refs[many:]
        copies = weight.copies(where, sources, held, sems)
        for group in copies:
            start_all(group)
        value = add_core(part, came)
        branch[...] = value
        total = two_cores((own, other)) + mods[2:3] * value
        middle[...] = total
        normed, _ = normalize(total)
        value = (normed * (1.0 + mods[4:5]) + mods[3:4]).astype(LOW)
        hidden[0] = value
        for side in range(2):
            x = lax.rem(where[3] + side, 2)
            wait_all(copies[side])
            before = dot(value, held[x])
            pre[x] = before.astype(LOW)
            act[x] = gelu(before).astype(LOW)

    dims = (count, features)
    return call(
        body,
        where,
        [(a, True) for a in (part, came, *rows, mods)] + [(w, False) for w in weight.arrays],
        [shape(dims, FULL), shape(dims, FULL), shape((1,) + dims, LOW)]
        + [shape((2, count, cols), LOW)] * 2,
        weight.scratch(),
        4 * count * features * cols,
        "norm_up",
    )


def down_part(where, act, weight):
    _, count, wide = act.shape
    many = len(weight.arrays)

    def body(where, act, *refs):
        sources, (out, held, sems) = refs[:many], refs[many:]
        copies = weight.copies(where, sources, held, sems)
        for group in copies:
            start_all(group)
        totals = []
        for side in range(2):
            place = lax.rem(where[3] + side, 2)
            wait_all(copies[side])
            total = dot(act[0], held[place, :wide]) + dot(act[1], held[place, wide:])
            totals.append(total[:, : weight.cols].astype(LOW))
        out[...] = jnp.concatenate(by_place(where[3] == 0, totals), axis=1)

    return call(
        body,
        where,
        [(act, True)] + [(w, False) for w in weight.arrays],
        [shape((count, 2 * weight.cols), LOW)],
        weight.scratch(),
        8 * count * wide * weight.cols,
        "down_part",
    )[0]


def finish(where, part, came, middle, mods):
    count, features = part.shape

    def body(where, part, came, middle, mods, mlp, out):
        total = add_core(part, came)
        mlp[...] = total
        size = count // 2
        out[...] = (middle[:size] + mods[5:6] * total[:size]).astype(LOW)

    return call(
        body,
        where,
        [(a, True) for a in (part, came, middle, mods)],
        [shape((count, features), FULL), shape((count // 2, features), LOW)],
        [],
        0,
        "finish",
    )


def column_sums(*values):
    sums = [jnp.sum(v, axis=0, keepdims=True) for v in values]
    fill = jnp.zeros((8 - len(sums), sums[0].shape[1]), FULL)
    return jnp.concatenate(sums + [fill], axis=0)


def mlp_back(where, grads, mods, pre, up, down):
    count, features = grads[0].shape
    count *= 2
    wide = pre.shape[-1]
    cols = down.cols
    many_up, many_down = len(up.arrays), len(down.arrays)

    def body(where, own, other, mods, pre, *refs):
        ups, downs = refs[:many_up], refs[many_up : many_up + many_down]
        grad_mlp, grad_pre, part, up_held, up_sems, down_held, down_sems = refs[many_up + many_down :]
        down_copies = down.copies(where, downs, down_held, down_sems)
        up_copies = up.copies(where, ups, up_held, up_sems)
        for group in down_copies + up_copies:
            start_all(group)
        scaled = (mods[5:6] * two_cores((own, other))).astype(LOW)
        sides = [scaled[:, s * cols : (s + 1) * cols] for s in range(2)]
        for s in range(2):
            grad_mlp[s] = sides[s]
        wait_all(down_copies[0] + down_copies[1])
        total = None
        for side in range(2):
            x = lax.rem(where[3] + side, 2)
            rows = pl.ds(pl.multiple_of(x * wide, 16), wide)
            grad_act = dot_nt(sides[0], down_held[0, rows, :cols]) + dot_nt(
                sides[1], down_held[1, rows, :cols]
            )
            value = (gelu_slope(pre[x].astype(FULL)) * grad_act).astype(LOW)
            grad_pre[x] = value
            wait_all(up_copies[side])
            piece = dot_nt(value, up_held[x])
            total = piece if total is None else total + piece
        part[...] = total.astype(LOW)

    return call(
        body,
        where,
        [(a, True) for a in (*grads, mods, pre)] + [(w, False) for w in up.arrays + down.arrays],
        [
            shape((2, count, cols), LOW),
            shape((2, count, wide), LOW),
            shape((count, features), LOW),
        ],
        up.scratch() + down.scratch(),
        8 * count * features * wide,
        "mlp_back",
    )


def attend_grad(
    where, part, came, grads, mods, middle, branch, mlp, out_weight, qkv, marks, head
):
    _, count, cols = qkv.shape
    heads = 2 * cols // (3 * head)
    factor = head ** (-0.5)
    features = part.shape[1]
    wide = features // 2
    size = count // 2

    def body(where, part, came, own, other, mods, middle, branch, mlp, out_weight, qkv, *refs):
        mask = None
        if marks is not None:
            mask = refs[0][...] == refs[1][...]
        grad_mid, grad_branch, sums, out = refs[-4:]
        incoming = two_cores((own, other))
        total = add_core(part, came)
        normed, inverse = normalize(middle[...])
        result = incoming + normalize_back(total * (1.0 + mods[4:5]), normed, inverse)
        grad_mid[...] = result
        sums[...] = column_sums(result * branch[...], total, total * normed, incoming * mlp[...])
        scaled = (mods[2:3] * result).astype(LOW)
        sides = [scaled[:, s * wide : (s + 1) * wide] for s in range(2)]
        for s in range(2):
            grad_branch[s] = sides[s]
        attended = dot_nt(sides[0], out_weight[0]) + dot_nt(sides[1], out_weight[1])
        attended = attended.astype(LOW)
        for block in range(2):
            rows = slice(block * size, (block + 1) * size)
            pieces = [None] * (3 * heads)
            for number in range(heads):
                grad = attended[rows, number * head : (number + 1) * head]
                query, key, value = head_slices(qkv, rows, number, heads, head)
                probs = probabilities(query, key, mask, factor)
                grad_probs = dot_nt(value, grad)
                delta = jnp.sum(grad_probs * probs, axis=0, keepdims=True)
                grad_scores = (probs * (grad_probs - delta)).astype(LOW)
                pieces[number] = (dot_tn(key, grad_scores).T * factor).astype(LOW)
                pieces[heads + number] = (dot(grad_scores, query) * factor).astype(LOW)
                pieces[2 * heads + number] = dot(probs.astype(LOW), grad).astype(LOW)
            per = 3 * heads // 2
            for x in range(2):
                out[x, rows] = jnp.concatenate(pieces[x * per : (x + 1) * per], axis=1)

    ins = [(a, True) for a in (part, came, *grads, mods, middle, branch, mlp, out_weight, qkv)]
    ins += [] if marks is None else [(m, True) for m in marks]
    return call(
        body,
        where,
        ins,
        [
            shape((count, features), FULL),
            shape((2, count, wide), LOW),
            shape((8, features), FULL),
            shape((2, count, cols), LOW),
        ],
        [],
        20 * heads * count * size * head,
        "attend_grad",
    )


def qkv_part(where, grad_qkv, weight, features):
    _, count, cols = grad_qkv.shape
    many = len(weight.arrays)

    def body(where, grad_qkv, *refs):
        sources, (out, held, sems) = refs[:many], refs[many:]
        copies = weight.copies(where, sources, held, sems)
        for group in copies:
            start_all(group)
        total = None
        for side in range(2):
            x = lax.rem(where[3] + side, 2)
            wait_all(copies[side])
            piece = dot_nt(grad_qkv[x], held[x, :, :cols])
            total = piece if total is None else total + piece
        out[...] = total.astype(LOW)

    return call(
        body,
        where,
        [(grad_qkv, True)] + [(w, False) for w in weight.arrays],
        [shape((count, features), LOW)],
        weight.scratch(),
        4 * count * features * cols,
        "qkv_part",
    )[0]


def finish_back(where, part, came, rows, mods, grad_mid):
    count, features = part.shape

    def body(where, part, came, own, other, mods, grad_mid, out, sums):
        total = add_core(part, came)
        normed, inverse = normalize(two_cores((own, other)))
        back = normalize_back(total * (1.0 + mods[1:2]), normed, inverse)
        sums[...] = column_sums(total, total * normed)
        size = count // 2
        out[...] = (grad_mid[:size] + back[:size]).astype(LOW)

    return call(
        body,
        where,
        [(a, True) for a in (part, came, *rows, mods, grad_mid)],
        [shape((count // 2, features), LOW), shape((8, features), FULL)],
        [],
        0,
        "finish_back",
    )


def weight_grad(where, left, right, tail, depth, cut):
    blocks, count, wide = left.shape
    rows = blocks * wide // (2 * depth)
    cols = right.shape[-1]
    operands = [left, right]
    scratch = [pltpu.VMEM((blocks * wide, count), LOW)]
    if tail is not None:
        size, thin = tail[0].shape[-1], tail[1].shape[-1] // 2
        operands += tail
        scratch.append(pltpu.VMEM((size, count), LOW))
        cols += thin
    many = len(operands)
    cuts = [(at, to) for at, to in ((0, cut), (cut, cols)) if to > at]

    def kernel(where, *refs):
        ins, outs, held = refs[:many], refs[many : -len(scratch)], refs[-len(scratch) :]
        z = pl.program_id(0)

        @pl.when(z == 0)
        def _():
            for source, flipped in zip(ins[::2], held):
                size = source.shape[-1]
                for block in range(source.shape[0]):
                    flipped[block * size : (block + 1) * size] = source[block].T

        chosen = []
        for flipped in held:
            size = flipped.shape[0] // depth
            chosen.append(flipped[pl.ds(pl.multiple_of(z * size, 16), size)])

        for turn, x in enumerate((1 - where[3], where[3])):
            value = dot(chosen[0], ins[1][x])
            value = [value[:rows], value[rows:]]
            if tail is not None:
                more = dot(chosen[1], ins[3][x])
                size = more.shape[0] // 2
                for y in range(2):
                    part = more[y * size : (y + 1) * size]
                    strips = jnp.concatenate([part[:, :thin], part[:, thin:]], axis=0)
                    value[y] = jnp.concatenate([value[y], strips], axis=1)
            own, other = by_place(where[1] == 0, value)
            for number, (at, to) in enumerate(cuts):
                outs[4 * number + 2 * turn][0] = other[:, at:to].astype(LOW)
                outs[4 * number + 2 * turn + 1][0] = own[:, at:to].astype(LOW)

    def whole(a):
        return pl.BlockSpec(a.shape, lambda i, s: (0,) * len(a.shape))

    widths = [to - at for at, to in cuts for _ in range(4)]
    return pl.pallas_call(
        kernel,
        out_shape=[shape((depth, rows, w), LOW) for w in widths],
        grid_spec=pltpu.PrefetchScalarGridSpec(
            num_scalar_prefetch=1,
            grid=(depth,),
            in_specs=[whole(a) for a in operands],
            out_specs=[pl.BlockSpec((1, rows, w), lambda i, s: (i, 0, 0)) for w in widths],
            scratch_shapes=scratch,
        ),
        compiler_params=pltpu.CompilerParams(vmem_limit_bytes=LIMIT),
        cost_estimate=TINY,
        name="weight_grad",
    )(where, *operands)


def add_all(where, *arrays):
    depth, rows, cols = arrays[0].shape

    def kernel(where, *refs):
        total = refs[0][...].astype(FULL)
        for ref in refs[1:-1]:
            total = total + ref[...].astype(FULL)
        refs[-1][...] = total.astype(LOW)

    moving = pl.BlockSpec((1, rows, cols), lambda i, s: (i, 0, 0))
    return pl.pallas_call(
        kernel,
        out_shape=shape((depth, rows, cols), LOW),
        grid_spec=pltpu.PrefetchScalarGridSpec(
            num_scalar_prefetch=1,
            grid=(depth,),
            in_specs=[moving] * len(arrays),
            out_specs=moving,
        ),
        compiler_params=pltpu.CompilerParams(vmem_limit_bytes=LIMIT),
        cost_estimate=TINY,
        name="add_all",
    )(where, *arrays)


def add_planes(where, *strips):
    depth, rows, _ = strips[0][0].shape
    count = len(strips[0])
    cols = sum(a.shape[-1] for a in strips[0])

    def body(where, *refs):
        ins, outs = refs[: count * len(strips)], refs[count * len(strips) :]
        for ahead, out in enumerate(outs):
            z = lax.rem(where[0] + ahead, depth)
            at = 0
            for number in range(count):
                total = ins[number][z].astype(FULL)
                for ref in ins[number + count :: count]:
                    total = total + ref[z].astype(FULL)
                wide = total.shape[-1]
                out[:, at : at + wide] = total.astype(out.dtype)
                at += wide

    return call(
        body,
        where,
        [(a, True) for group in strips for a in group],
        [shape((rows, cols), FULL)] + [shape((rows, cols), LOW)] * (depth - 1),
        [],
        0,
        "add_planes",
    )


def add_planes_last(where, *planes):
    def body(where, *refs):
        total = refs[0][...]
        for ref in refs[1:-1]:
            total = total + ref[...].astype(FULL)
        refs[-1][...] = total

    outs = [shape(planes[0].shape, FULL)]
    return call(body, where, [(p, True) for p in planes], outs, [], 0, "add_planes_last")[0]


def part_rows(where, totals, cols):
    rows = totals[0].shape[0]
    wide = sum(t.shape[1] for t in totals)
    part, thin = rows // 2, wide - cols

    def body(where, *refs):
        ins, outs = refs[: len(totals)], refs[len(totals) :]
        total = jnp.concatenate([ref[...].astype(FULL) for ref in ins], axis=1)
        mine, theirs = by_place(where[2] == 0, [total[:part, :cols], total[part:, :cols]])
        if thin:
            outs[0][...] = jnp.concatenate([total[:part, cols:], total[part:, cols:]], axis=1)
        outs[-2][...] = mine
        outs[-1][...] = theirs.astype(LOW)

    outs = [shape((part, cols), FULL), shape((part, cols), LOW)]
    if thin:
        outs.insert(0, shape((part, 2 * thin), FULL))
    return call(body, where, [(t, True) for t in totals], outs, [], 0, "part_rows")


def interleave(where, mine, theirs, width):
    rows, cols = mine.shape

    def body(where, mine, theirs, out):
        both = by_place(where[2] == 0, [mine[...], theirs[...].astype(FULL)])
        groups = []
        for at in range(0, cols, width):
            groups += [b[:, at : at + width] for b in both]
        out[...] = jnp.concatenate(groups, axis=1)

    return call(
        body,
        where,
        [(mine, True), (theirs, True)],
        [shape((rows, 2 * cols), FULL)],
        [],
        0,
        "interleave",
    )[0]


def deal(where, shards, widths):
    rows = shards[0].shape[0]
    cols = sum(a.shape[1] for a in shards) // 2

    def body(where, *refs):
        own, other = refs[-2:]
        halves = [[], []]
        for ref, width in zip(refs, widths):
            value = ref[...]
            for number in range(value.shape[1] // width):
                halves[number % 2].append(value[:, number * width : (number + 1) * width])
        pair = [jnp.concatenate(h, axis=1) for h in halves]
        own[...], other[...] = by_place(where[2] == 0, pair)

    return call(
        body,
        where,
        [(a, True) for a in shards],
        [shape((rows, cols), LOW)] * 2,
        [],
        0,
        "deal",
    )


def pack(where, own, got, outs, downs, cols):
    part = own.shape[0]
    rows = 2 * part
    thin = outs[0].shape[1] // 2
    wide = downs[0].shape[1]
    padded = -(-wide // 128) * 128
    count = downs[0].shape[0] // rows
    first = cols[0] + thin

    def body(where, own, got, out_s, out_t, down_s, down_t, qkv_s, mlp_s, packed):
        pair = by_place(where[2] == 0, [own[...].astype(FULL), got[...].astype(FULL)])
        both = jnp.concatenate(pair, axis=0)

        def strips(ref):
            value = ref[...].astype(FULL)
            return jnp.concatenate([value[:, :thin], value[:, thin:]], axis=0)

        def put_down(to, lane, down):
            for k in range(count):
                to[:, lane : lane + wide] = down[k * rows : (k + 1) * rows]
                if padded > wide:
                    to[:, lane + wide : lane + padded] = jnp.zeros((rows, padded - wide), LOW)
                lane += padded

        at = cols[0] + cols[1]
        qkv_s[...] = jnp.concatenate([both[:, : cols[0]], strips(out_s)], axis=1).astype(LOW)
        mlp_s[:, : cols[1]] = both[:, cols[0] : at].astype(LOW)
        put_down(mlp_s, cols[1], down_s)
        qkv_t = jnp.concatenate([both[:, at : at + cols[0]], strips(out_t)], axis=1)
        packed[:, :first] = qkv_t.astype(LOW)
        packed[:, first : first + cols[1]] = both[:, at + cols[0] :].astype(LOW)
        put_down(packed, first + cols[1], down_t)

    mlp = cols[1] + count * padded
    return call(
        body,
        where,
        [(a, True) for a in (own, got, *outs, *downs)],
        [shape((rows, first), LOW), shape((rows, mlp), LOW), shape((rows, first + mlp), LOW)],
        [],
        0,
        "pack",
    )


class Grid:
    def __init__(self, patch, seq, patch_axes, seq_axis):
        self.patch_axes, self.seq_axis = patch_axes, seq_axis
        self.every = (patch_axes if isinstance(patch_axes, tuple) else (patch_axes,)) + (seq_axis,)
        self.chips = self.every[:2] + (seq_axis,)
        self.patch, self.seq = patch, seq
        self.depth = patch // 4
        where = lax.axis_index(patch_axes)
        self.place = where
        self.core = where % 2
        self.y = (where // 2) % 2
        self.z = where // 4
        self.x = lax.axis_index(seq_axis)

    def moves(self, step):
        pairs = []
        for p in range(self.patch):
            for x in range(self.seq):
                z, y, c = p // 4, (p // 2) % 2, p % 2
                z2, y2, c2, x2 = step(z, y, c, x)
                pairs.append((p * self.seq + x, ((z2 * 2 + y2) * 2 + c2) * self.seq + x2))
        return pairs

    def send(self, array, step):
        return lax.ppermute(array, self.every, self.moves(step))

    def flip_core(self, array):
        return self.send(array, lambda z, y, c, x: (z, y, 1 - c, x))

    def flip_y(self, array):
        return self.send(array, lambda z, y, c, x: (z, 1 - y, c, x))

    def shift_x(self, array, by):
        return self.send(array, lambda z, y, c, x: (z, y, c, (x + by) % self.seq))

    def shift_z(self, array, by):
        return self.send(array, lambda z, y, c, x: ((z + by) % self.depth, y, c, x))

    def xor_patch(self, array, bit):
        pairs = [
            (p * self.seq + x, (p ^ bit) * self.seq + x)
            for p in range(self.patch)
            for x in range(self.seq)
        ]
        return lax.ppermute(array, self.every, pairs)

    def bits(self):
        bit = self.patch // 2
        while bit:
            yield bit
            bit //= 2

    def sum_patch(self, array):
        for bit in self.bits():
            array = array + self.xor_patch(array, bit)
        return array

    def join_patch(self, array, other, bit):
        mine_first = (self.place // bit) % 2 == 0
        return jnp.where(
            mine_first, jnp.concatenate([array, other]), jnp.concatenate([other, array])
        )

    def all_seq(self, array):
        return [array] + [self.shift_x(array, -j) for j in range(1, self.seq)]


class Flight:
    pass


class Split:
    def __init__(self, grid, head, group, token):
        self.grid = grid
        self.head, self.group = head, group
        self.up_cols = group * grid.patch // 4
        self.split_cut = 5 * 128
        self.token = token
        self.strict = True
        self.flights = []
        self.strict = True
        self.where = jnp.stack([grid.z, grid.y, grid.core, grid.x]).astype(jnp.int32)

    @staticmethod
    def fits(patch, seq, frames, features, hidden):
        return (
            patch == HEADS
            and patch == frames
            and seq == 2
            and features % (2 * patch) == 0
            and hidden % patch == 0
            and (2 * features // patch) % 16 == 0
            and hidden == 2 * 2 * features
            and (hidden // patch) % 32 == 0
        )


    def tie(self, *arrays):
        *arrays, self.token = lax.optimization_barrier((*arrays, self.token))
        return arrays[0] if len(arrays) == 1 else arrays

    def run(self, kernel, first, *rest):
        if isinstance(first, (list, tuple)):
            head, *tail = first
            if isinstance(head, tuple):
                first = [(self.tie(head[0]), *head[1:]), *tail]
            else:
                first = [self.tie(head), *tail]
        else:
            first = self.tie(first)
        result = kernel(self.where, first, *rest)
        if not self.strict:
            self.token = result[-1] if isinstance(result, (list, tuple)) else result
            return result
        if isinstance(result, (list, tuple)):
            return self.tie(*result) if len(result) > 1 else [self.tie(result[0])]
        return self.tie(result)

    def first(self, array, x_first):
        return self.grid.shift_x(array, 1) if x_first else self.grid.flip_y(array)

    def prepare(self, spatial, temporal):
        own, other = deal(
            self.where,
            [spatial[0], spatial[2], temporal[0], temporal[2]],
            [self.head, self.group] * 2,
        )
        got = self.grid.flip_core(other)
        cols = (spatial[0].shape[1] // 2, spatial[2].shape[1] // 2)
        outs, downs = [spatial[1], temporal[1]], [spatial[3], temporal[3]]
        return self.run(pack, own, got, outs, downs, cols)

    def gather_z(self, piece):
        piece = self.tie(piece)
        moves = [partial(self.grid.shift_z, by=-j) for j in range(1, self.grid.depth)]
        return piece, [self.fly(piece, move) for move in moves]

    def fly(self, array, move):
        flight = Flight()
        flight.value = move(self.tie(array))
        self.flights.append(flight)
        return flight

    def land(self, *chosen):
        chosen = chosen or tuple(self.flights)
        arrived = self.tie(*[flight.value for flight in chosen], self.token)
        for flight, value in zip(chosen, arrived):
            flight.value = value
        self.flights = [f for f in self.flights if not any(f is c for c in chosen)]

    def move_first(self, x_first):
        return partial(self.first, x_first=x_first)

    def split_rows(self, totals, cols, width):
        *rest, mine, theirs = self.run(part_rows, totals, cols)
        flight = self.fly(theirs, self.grid.flip_core)
        yield
        yield [self.run(interleave, mine, flight.value, width)] + rest

    def across_z(self, array):
        return lax.psum_scatter(array, self.grid.chips[0], scatter_dimension=0, tiled=False)

    def both(self, array):
        return [array, self.grid.flip_core(array)]

    def forward(self, rows, mods, mod_steps, shards, down_shape, marks, to_frames, to_patches):
        grid, head = self.grid, self.head
        qkv_s, mlp_s, packed = shards
        depth, count = grid.depth, qkv_s.shape[0]
        cols = qkv_s.shape[1], self.up_cols
        padded = (mlp_s.shape[1] - cols[1]) * count // down_shape[0]
        cut = self.split_cut
        chunk = 3 * head * HEADS // 4

        def halved(strips, width, placed):
            return [
                (strip.buffers, strip.x_first, placed, 0, 0, count, lane, lanes)
                for strip, lane, lanes in zip(strips, (0, cut), (cut, width - cut))
            ]

        def stacked(pieces, cuts):
            own, flights = pieces
            self.land(*flights)
            pieces = [own] + [flight.value for flight in flights]
            parts = [jnp.stack([p[:, at:to] for p in pieces]) for at, to in zip(cuts, cuts[1:])]
            parts = self.tie(*parts)
            return [Arriving(self, part, k % 2 == 0) for k, part in enumerate(parts)]

        rows = self.fly(rows, to_frames)
        pieces = self.gather_z(qkv_s)
        list(mod_steps)
        mods = mods()
        one = stacked(pieces, [0, cut, cols[0]])
        for strip in one:
            strip.first()
        self.land(rows)
        rows = self.both(rows.value)
        pieces = self.gather_z(mlp_s)
        for strip in one:
            strip.second()
        self.land(*[strip.flight for strip in one])
        two = up, down = stacked(pieces, [0, cols[1], mlp_s.shape[1]])
        held_t = lax.all_gather(self.tie(packed), grid.chips[0], axis=0)
        for strip in two:
            strip.first()
        qkv_w = Weight(depth, count, cols[0], halved(one, cols[0], False))
        hidden_one, out_w, qkv = self.run(norm_qkv, rows, mods[0], qkv_w, chunk)
        attended, part = self.run(attend_out, qkv, out_w, None, head)
        came = self.fly(part, grid.flip_core)
        for strip in two:
            strip.second()
        self.land(came)
        held_t = self.tie(held_t)
        cuts = [0, cols[0], cols[0] + cols[1]]
        cuts += [cuts[-1] + padded, cuts[-1] + 2 * padded]
        strips = [self.tie(held_t[..., at:to]) for at, to in zip(cuts, cuts[1:])]
        strips = [Arriving(self, s, k % 2 == 0) for k, s in enumerate(strips)]
        for strip in strips[:2]:
            strip.first()
        self.land(*[strip.flight for strip in two])
        up_w = Weight(
            depth, count, cols[1], [(up.buffers, True, False, 0, 0, count, 0, cols[1])]
        )
        down_w = Weight(
            depth,
            *down_shape,
            [
                (down.buffers, False, False, k * padded, k * count, count, 0, padded)
                for k in range(down_shape[0] // count)
            ],
        )
        branch, middle, hidden_two, pre, act = self.run(
            norm_up, part, came.value, rows, mods[0], up_w
        )
        part = self.run(down_part, act, down_w)
        came = self.fly(part, grid.flip_core)
        for strip in strips[:2]:
            strip.second()
        for strip in strips[2:]:
            strip.first()
        self.land(came)
        mlp, result = self.run(finish, part, came.value, middle, mods[0])
        spatial = (
            (mods[0], None, rows),
            (qkv_w, out_w, up_w, down_w),
            (hidden_one, qkv, attended, branch, middle, hidden_two, pre, act, mlp),
        )

        for strip in strips[2:]:
            strip.second()
        moved = self.fly(result, to_patches)
        self.land(moved)
        rows = [moved.value, self.fly(moved.value, grid.flip_core)]
        self.land(rows[1])
        rows[1] = rows[1].value
        self.land(*[strip.flight for strip in strips[:2]])
        early, late = strips[:2]
        qkv_w = Weight(
            depth, count, cols[0], [(early.buffers, True, True, 0, 0, count, 0, cols[0])]
        )
        up_w = Weight(
            depth, count, cols[1], [(late.buffers, False, True, 0, 0, count, 0, cols[1])]
        )
        hidden_one, out_w, qkv = self.run(norm_qkv, rows, mods[1], qkv_w, chunk)
        attended, part = self.run(attend_out, qkv, out_w, marks, head)
        came = self.fly(part, grid.flip_core)
        self.land(came)
        branch, middle, hidden_two, pre, act = self.run(
            norm_up, part, came.value, rows, mods[1], up_w
        )
        self.land()
        down_w = Weight(
            depth,
            *down_shape,
            [
                (strip.buffers, strip.x_first, True, 0, k * count, count, 0, padded)
                for k, strip in enumerate(strips[2:])
            ],
        )
        part = self.run(down_part, act, down_w)
        came = self.fly(part, grid.flip_core)
        self.land()
        mlp, result = self.run(finish, part, came.value, middle, mods[1])
        temporal = (
            (mods[1], marks, rows),
            (qkv_w, out_w, up_w, down_w),
            (hidden_one, qkv, attended, branch, middle, hidden_two, pre, act, mlp),
        )
        return result, spatial, temporal

    def grads_of(self, left, right, tail, cut, orders):
        quads = self.run(weight_grad, left, right, tail, self.grid.depth, cut)
        return [Strip(self, quads[4 * k : 4 * k + 4], order) for k, order in enumerate(orders)]

    def backward(self, spatial, temporal, grad, move, move_back, condition_steps):
        start = self.token
        self.strict = False
        head, flip = self.head, self.grid.flip_core
        (mods, marks, rows), (qkv_w, out_w, up_w, down_w), saved = temporal
        hidden_one, qkv, attended, branch, middle, hidden_two, pre, act, mlp = saved
        features = grad.shape[-1]
        wide, half = 2 * features // 2, features // 2
        chunk = 3 * half // 2
        grads = self.both(grad)
        grad_mlp, grad_pre, part = self.run(mlp_back, grads, mods, pre, up_w, down_w)
        came = self.fly(part, flip)
        (up_t,) = self.grads_of(hidden_two, grad_pre, None, wide, [True])
        self.land()

        up_t.first(0)
        (down_t,) = self.grads_of(act, grad_mlp, None, 0, [False])
        grad_mid, grad_branch, sums_two, grad_qkv = self.run(
            attend_grad,
            part,
            came.value,
            grads,
            mods,
            middle,
            branch,
            mlp,
            out_w,
            qkv,
            marks,
            head,
        )
        self.land()

        up_t.first(1)
        down_t.first(0)
        part = self.run(qkv_part, grad_qkv, qkv_w, features)
        came = self.fly(part, flip)
        (qkv_t,) = self.grads_of(hidden_one, grad_qkv, [attended, grad_branch], wide, [True])
        self.land()

        down_t.first(1)
        grad, sums_one = self.run(finish_back, part, came.value, rows, mods, grad_mid)
        mods_t = jnp.concatenate([sums_one[:2], sums_two[:4]], axis=0).reshape(1, -1)
        moved = self.fly(grad, move)
        up_t.second()
        self.land()

        qkv_t.first(0)
        grads = [moved.value, self.fly(moved.value, flip)]
        down_t.add_second()
        self.land()
        grads[1] = grads[1].value

        qkv_t.first(1)
        up_t.fly_second()
        (mods, marks, rows), (qkv_w, out_w, up_w, down_w), saved = spatial
        hidden_one, qkv, attended, branch, middle, hidden_two, pre, act, mlp = saved
        grad_mlp, grad_pre, part = self.run(mlp_back, grads, mods, pre, up_w, down_w)
        self.land()

        came = self.fly(part, flip)
        down_t.fly_second()
        (up_s,) = self.grads_of(hidden_two, grad_pre, None, wide, [False])
        (down_s,) = self.grads_of(act, grad_mlp, None, half, [True])
        up_t.total()
        self.land()

        up_s.first(0)
        down_s.first(0)
        up_z = self.across_z(up_t.sum)
        grad_mid, grad_branch, sums_two, grad_qkv = self.run(
            attend_grad,
            part,
            came.value,
            grads,
            mods,
            middle,
            branch,
            mlp,
            out_w,
            qkv,
            marks,
            head,
        )
        qkv_t.add_second()
        self.land()

        up_s.first(1)
        down_s.first(1)
        (early, late) = self.grads_of(
            hidden_one, grad_qkv, [attended, grad_branch], self.split_cut, [True, False]
        )
        part = self.run(qkv_part, grad_qkv, qkv_w, features)
        came = self.fly(part, flip)
        down_t.total()
        down_z = self.across_z(down_t.sum)
        self.land()

        early.first(0)
        late.first(0)
        qkv_t.fly_second()
        grad, sums_one = self.run(finish_back, part, came.value, rows, mods, grad_mid)
        mods_s = jnp.concatenate([sums_one[:2], sums_two[:4]], axis=0).reshape(1, -1)
        up_s.add_second()
        down_s.add_second()
        self.land()

        early.first(1)
        late.first(1)
        up_s.fly_second()
        down_s.fly_second()
        qkv_t.total()
        qkv_z = self.across_z(qkv_t.sum)
        early.add_second()
        late.add_second()
        self.land()

        early.fly_second()
        late.fly_second()
        up_s.total()
        up_sz = self.across_z(up_s.sum)
        down_s.total()
        down_sz = self.across_z(down_s.sum)
        self.land()
        self.strict = True
        self.token, _ = lax.optimization_barrier((start, self.token))
        chain = Chain(self, condition_steps(mods_s, mods_t))
        own, *planes = self.run(
            add_planes,
            [early.near[1], late.near[1]],
            [early.came[1].value, late.came[1].value],
            [early.last.value, late.last.value],
        )
        planes = [
            self.fly(plane, partial(self.grid.shift_z, by=j + 1)) for j, plane in enumerate(planes)
        ]
        for _ in range(4):
            chain.advance()
        up_t = self.split_rows([up_z], wide, self.group)
        next(up_t)
        self.land(self.flights[-1])
        (up_t,) = next(up_t)
        chain.advance()
        qkv_t = self.split_rows([qkv_z], chunk, head)
        next(qkv_t)
        self.land(self.flights[-1])
        qkv_t, out_t = next(qkv_t)
        chain.advance()
        tokens = self.fly(grad, move_back)
        chain.advance()
        self.land(*planes)
        qkv_sz = self.run(add_planes_last, own, *[plane.value for plane in planes])
        qkv_s = self.split_rows([qkv_sz], chunk, head)
        next(qkv_s)
        chain.advance()
        up_s = self.split_rows([up_sz], wide, self.group)
        next(up_s)
        chain.advance()
        self.land()
        qkv_s, out_s = next(qkv_s)
        (up_s,) = next(up_s)
        down_t, down_s = down_z.astype(FULL), down_sz.astype(FULL)
        grads = (qkv_s, out_s, up_s, down_s), (qkv_t, out_t, up_t, down_t)
        return tokens.value, chain.result, *grads


class Chain:
    def __init__(self, plan, steps):
        self.plan, self.steps = plan, steps
        self.flight = plan.fly(*next(steps))

    def advance(self):
        self.plan.land(self.flight)
        request = self.steps.send(self.flight.value)
        if isinstance(request[1], partial):
            self.flight = self.plan.fly(*request)
        else:
            self.result = request


class Arriving:
    def __init__(self, plan, held, x_first):
        self.plan, self.held, self.x_first = plan, held, x_first

    def first(self):
        self.flight = self.plan.fly(self.held, self.plan.move_first(self.x_first))

    def second(self):
        self.plan.land(self.flight)
        self.held = self.plan.tie(jnp.stack([self.held, self.flight.value]))
        self.flight = self.plan.fly(self.held, self.plan.move_first(not self.x_first))

    @property
    def buffers(self):
        return [self.held, self.flight.value]


class Strip:
    def __init__(self, plan, quads, x_first):
        self.plan, self.x_first = plan, x_first
        far = [quads[0], quads[1] if x_first else quads[2]]
        self.near = [quads[2] if x_first else quads[1], quads[3]]
        self.far, self.came = far, [None, None]

    def first(self, turn):
        self.came[turn] = self.plan.fly(self.far[turn], self.plan.move_first(self.x_first))

    def add_second(self):
        self.send = self.plan.run(add_all, self.near[0], self.came[0].value)

    def fly_second(self):
        self.last = self.plan.fly(self.send, self.plan.move_first(not self.x_first))

    def second(self):
        self.add_second()

    def total(self):
        self.sum = self.plan.run(add_all, self.near[1], self.came[1].value, self.last.value)


class WholeWeights:
    def __init__(self, grid, features, hidden):
        self.features, self.hidden = features, hidden

    def gather(self, local):
        wide = lax.all_gather(local, "seq", axis=1, tiled=True)
        return lax.all_gather(wide, "patch", axis=0, tiled=True)

    def fetch(self, spatial, temporal):
        return [[tuple(self.gather(w) for w in block)] for block in (spatial, temporal)]

    def scatter(self, grad):
        rows = lax.psum_scatter(grad.astype(LOW), "patch", scatter_dimension=0, tiled=True)
        return lax.psum_scatter(rows, "seq", scatter_dimension=1, tiled=True).astype(FULL)

    def reduce_mlp(self, hidden, grad_pre, activated, grad_mlp, flip):
        return (
            self.scatter(matmul_tn(hidden, grad_pre[0])),
            self.scatter(matmul_tn(activated[0], grad_mlp)),
        )

    def reduce_out(self, attended, grad_branch, flip):
        return self.scatter(matmul_tn(attended[0], grad_branch))

    def reduce_qkv(self, hidden, grad_qkv, flip):
        return self.scatter(matmul_tn(hidden, grad_qkv[0]))


def attention(queries, keys, mask, factor):
    scores = jnp.einsum("bphd,bkhd->bhpk", queries, keys, preferred_element_type=FULL) * factor
    if mask is not None:
        scores = jnp.where(mask, scores, -1e30)
    top = jnp.max(scores, axis=-1, keepdims=True)
    weights = jnp.exp(scores - top)
    return weights / jnp.sum(weights, axis=-1, keepdims=True)


def attend(qkv, batch, mask, head, share):
    rows = qkv.reshape(batch, -1, 3, qkv.shape[-1] // (3 * head), head)
    keys, values = share(rows[:, :, 1]), share(rows[:, :, 2])
    probs = attention(rows[:, :, 0], keys, mask, head ** (-0.5)).astype(LOW)
    mixed = jnp.einsum("bhpk,bkhd->bphd", probs, values, preferred_element_type=FULL)
    return mixed.reshape(qkv.shape[0], -1).astype(LOW)


def attend_back(grad, qkv, batch, mask, head, share, share_back):
    factor = head ** (-0.5)
    heads = qkv.shape[-1] // (3 * head)
    rows = qkv.reshape(batch, -1, 3, heads, head)
    grad_rows = grad.reshape(batch, -1, heads, head)
    queries, keys, values = rows[:, :, 0], share(rows[:, :, 1]), share(rows[:, :, 2])
    probs = attention(queries, keys, mask, factor)
    grad_probs = jnp.einsum("bphd,bkhd->bhpk", grad_rows, values, preferred_element_type=FULL)
    delta = jnp.sum(grad_probs * probs, axis=-1, keepdims=True)
    grad_scores = (probs * (grad_probs - delta)).astype(LOW)
    grad_queries = (
        jnp.einsum("bhpk,bkhd->bphd", grad_scores, keys, preferred_element_type=FULL) * factor
    )
    grad_keys = (
        jnp.einsum("bhpk,bphd->bkhd", grad_scores, queries, preferred_element_type=FULL) * factor
    )
    grad_values = jnp.einsum(
        "bhpk,bphd->bkhd", probs.astype(LOW), grad_rows, preferred_element_type=FULL
    )
    joined = jnp.stack(
        [grad_queries, share_back(grad_keys), share_back(grad_values)], axis=2
    )
    return joined.reshape(qkv.shape[0], -1).astype(LOW)


def total_parts(parts):
    total = parts[0]
    for part in parts[1:]:
        total = total + part
    return total


def block_forward(residual, pieces, parts, mix):
    normed_one, inverse_one = normalize(residual)
    hidden_one = (normed_one * (1.0 + pieces[1]) + pieces[0]).astype(LOW)
    qkv = [matmul(hidden_one, part[0]).astype(LOW) for part in parts]
    attended = [mix(rows) for rows in qkv]
    branch = total_parts([matmul(a, part[1]) for a, part in zip(attended, parts)])
    middle = residual + pieces[2] * branch
    normed_two, inverse_two = normalize(middle)
    hidden_two = (normed_two * (1.0 + pieces[4]) + pieces[3]).astype(LOW)
    pre = [matmul(hidden_two, part[2]) for part in parts]
    activated = [jax.nn.gelu(v, approximate=True).astype(LOW) for v in pre]
    mlp = total_parts([matmul(a, part[3]) for a, part in zip(activated, parts)])
    result = middle + pieces[5] * mlp
    saved = (
        normed_one,
        inverse_one,
        hidden_one,
        qkv,
        attended,
        branch,
        normed_two,
        inverse_two,
        hidden_two,
        pre,
        activated,
        mlp,
    )
    return result, saved


def block_backward(incoming, pieces, parts, saved, mix_back, weights, groups, flip):
    (
        normed_one,
        inverse_one,
        hidden_one,
        qkv,
        attended,
        branch,
        normed_two,
        inverse_two,
        hidden_two,
        pre,
        activated,
        mlp,
    ) = saved
    grad_mlp = (pieces[5] * incoming).astype(LOW)
    grad_pre = []
    for part, v in zip(parts, pre):
        _, back = jax.vjp(partial(jax.nn.gelu, approximate=True), v)
        grad_pre.append(back(matmul_nt(grad_mlp, part[3]))[0].astype(LOW))
    grad_up, grad_down = weights.reduce_mlp(hidden_two, grad_pre, activated, grad_mlp, flip)
    grad_hidden_two = total_parts([matmul_nt(g, part[2]) for g, part in zip(grad_pre, parts)])
    grad_middle = incoming + normalize_back(
        grad_hidden_two * (1.0 + pieces[4]), normed_two, inverse_two
    )
    grad_branch = (pieces[2] * grad_middle).astype(LOW)
    grad_out = weights.reduce_out(attended, grad_branch, flip)
    grad_attended = [matmul_nt(grad_branch, part[1]).astype(LOW) for part in parts]
    grad_qkv_rows = [mix_back(g, rows) for g, rows in zip(grad_attended, qkv)]
    grad_qkv = weights.reduce_qkv(hidden_one, grad_qkv_rows, flip)
    grad_hidden_one = total_parts(
        [matmul_nt(g, part[0]) for g, part in zip(grad_qkv_rows, parts)]
    )
    grad_residual = grad_middle + normalize_back(
        grad_hidden_one * (1.0 + pieces[1]), normed_one, inverse_one
    )
    sums = [
        jnp.sum(v.reshape(groups, -1, v.shape[-1]), axis=1)
        for v in (
            grad_hidden_one,
            grad_hidden_one * normed_one,
            grad_middle * branch,
            grad_hidden_two,
            grad_hidden_two * normed_two,
            incoming * mlp,
        )
    ]
    grad_mods = jnp.concatenate(sums, axis=-1)
    return grad_residual, grad_mods, (grad_qkv, grad_out, grad_up, grad_down)


def per_device(
    patch,
    seq,
    patch_axes,
    seq_axis,
    tokens,
    cotangent,
    class_ids,
    timesteps,
    segments,
    class_table,
    mod_spatial,
    qkv_spatial,
    out_spatial,
    up_spatial,
    down_spatial,
    mod_temporal,
    qkv_temporal,
    out_temporal,
    up_temporal,
    down_temporal,
):
    groups, frames, patch_rows, features = tokens.shape
    row_count = groups * frames * patch_rows
    head = features // HEADS
    hidden = up_spatial.shape[1] * seq
    grid = Grid(patch, seq, patch_axes, seq_axis)
    split = groups == 1 and Split.fits(patch, seq, frames, features, hidden)

    ways = max(1, patch // frames)
    subgroups = None
    if ways > 1:
        subgroups = [[a * ways + b for a in range(frames)] for b in range(ways)]

    def to_frames(array):
        moved = lax.all_to_all(
            array.reshape(groups, frames, patch_rows, features),
            patch_axes,
            split_axis=1,
            concat_axis=2,
            tiled=True,
            axis_index_groups=subgroups,
        )
        return moved.reshape(row_count, features)

    own_frames = max(1, frames // patch)

    def to_patches(array):
        moved = lax.all_to_all(
            array.reshape(groups, own_frames, -1, features),
            patch_axes,
            split_axis=2,
            concat_axis=1,
            tiled=True,
            axis_index_groups=subgroups,
        )
        return moved.reshape(row_count, features)

    def sharers(by):
        return [
            (a * ways + b, a * ways + (b + by) % ways)
            for a in range(patch // ways)
            for b in range(ways)
        ]

    def share_frame(array):
        if ways == 1:
            return array
        return jnp.concatenate(
            [array] + [lax.ppermute(array, patch_axes, sharers(j)) for j in range(1, ways)], axis=1
        )

    def share_frame_back(array):
        if ways == 1:
            return array
        cut = jnp.split(array, ways, axis=1)
        total = cut[0]
        for j in range(1, ways):
            total = total + lax.ppermute(cut[j], patch_axes, sharers(-j))
        return total

    whose = [jnp.stack([class_ids, timesteps])]
    whose += [grid.shift_x(whose[0], -j) for j in range(1, seq)]
    every_class = [w[0] for w in whose]
    conditions = []
    for chosen, times in whose:
        one_hot = (
            chosen[:, None] == jnp.arange(class_table.shape[0], dtype=jnp.int32)[None, :]
        ).astype(LOW)
        conditions.append(matmul(one_hot, class_table) + time_features(times, features))
    cond_low = [jax.nn.silu(c).astype(LOW) for c in conditions]
    mod_rows = features // patch
    first_row = grid.place * mod_rows
    cond_own = [lax.dynamic_slice_in_dim(c, first_row, mod_rows, axis=1) for c in cond_low]
    modulation = []

    def mod_steps(hold):
        together = jnp.concatenate(cond_own)
        mods = jnp.stack([matmul(together, mod_spatial), matmul(together, mod_temporal)], axis=1)
        for bit in grid.bits():
            mods = hold(mods + grid.xor_patch(mods, bit))
            yield
        mods = mods.reshape(seq, groups, 2, -1).transpose(0, 2, 1, 3)
        received = [mods[0]] + [grid.shift_x(mods[j], j) for j in range(1, seq)]
        ordered = in_order(received[:1] + received[:0:-1], grid.x)
        modulation.append(hold(jnp.concatenate(ordered, axis=-1)))
        yield

    width = mod_spatial.shape[1]

    def outer(columns):
        return lax.dot_general(
            jnp.concatenate(cond_own).astype(FULL),
            columns,
            (((0,), (0,)), ((), ())),
            precision=PRECISE,
            preferred_element_type=FULL,
        )

    def condition_part(columns, mod):
        return lax.dot_general(
            columns,
            mod.astype(FULL),
            (((1,), (1,)), ((), ())),
            precision=PRECISE,
            preferred_element_type=FULL,
        )

    def condition_steps(spatial_sums, temporal_sums, own_class):
        sums = jnp.stack([spatial_sums, temporal_sums])
        for bit in grid.bits():
            if split and bit == 1:
                continue
            sums = sums + (yield sums, partial(grid.xor_patch, bit=bit))
        sums = sums.reshape(2, groups, seq, width)
        columns = [pick(sums, 2, grid.x)]
        for j in range(1, seq):
            away = pick(sums, 2, (grid.x - j) % seq)
            columns.append((yield away, partial(grid.shift_x, by=-j)))
        columns = jnp.concatenate(columns, axis=1)
        parts = condition_part(columns[0], mod_spatial) + condition_part(columns[1], mod_temporal)
        parts = parts.reshape(seq, groups, mod_rows)
        total = parts
        for j in range(1, seq):
            total = total + jnp.roll((yield parts, partial(grid.shift_x, by=j)), j, axis=0)
        total = total[None]
        bit = 1
        while bit < patch:
            total = grid.join_patch(total, (yield total, partial(grid.xor_patch, bit=bit)), bit)
            bit *= 2
        grad_condition = total.transpose(1, 2, 0, 3).reshape(seq * groups, features)
        _, silu_back = jax.vjp(jax.nn.silu, jnp.concatenate(conditions))
        every_hot = (
            jnp.concatenate([own_class()] + every_class[1:])[:, None]
            == jnp.arange(class_table.shape[0], dtype=jnp.int32)[None, :]
        ).astype(FULL)
        grad_class_table = lax.dot_general(
            every_hot,
            silu_back(grad_condition)[0],
            (((0,), (0,)), ((), ())),
            precision=PRECISE,
            preferred_element_type=FULL,
        )
        yield grad_class_table, outer(columns[0]), outer(columns[1])

    def conditions_at_once(spatial_sums, temporal_sums):
        steps = condition_steps(spatial_sums, temporal_sums, lambda: class_ids)
        request = next(steps)
        while isinstance(request[1], partial):
            request = steps.send(request[1](request[0]))
        return request


    spatial_shards = (qkv_spatial, out_spatial, up_spatial, down_spatial)
    temporal_shards = (qkv_temporal, out_temporal, up_temporal, down_temporal)
    span = frames * patch_rows
    patch_of = jnp.arange(span, dtype=jnp.int32) % patch_rows
    place_of = jnp.repeat(segments, patch_rows, axis=1) * patch_rows + patch_of[None, :]

    if split:
        plan = Split(grid, head, hidden // patch, whose[0])
        hold = plan.tie
        marks = (place_of.reshape(-1, 1), place_of.reshape(1, -1))
        shards = plan.prepare(spatial_shards, temporal_shards)
        steps = mod_steps(hold)
        for _ in range(2):
            next(steps)

        def mods_of():
            return [
                jnp.pad(modulation[-1][block].reshape(6, features), ((0, 2), (0, 0)))
                for block in range(2)
            ]

        result, spatial_state, temporal_state = plan.forward(
            tokens,
            mods_of,
            steps,
            shards,
            down_spatial.shape,
            marks,
            to_frames,
            to_patches,
        )
        out_tokens = result.reshape(tokens.shape)
        grad_spatial_in, condition_grads, spatial_grads, temporal_grads = plan.backward(
            spatial_state,
            temporal_state,
            cotangent.reshape(row_count, features),
            to_frames,
            to_patches,
            lambda s, t: condition_steps(s, t, lambda: plan.token[0]),
        )
        grad_tokens = grad_spatial_in.astype(FULL).reshape(tokens.shape)
    else:
        weights = WholeWeights(grid, features, hidden)
        list(mod_steps(lambda v: v))

        def pieces_of(block):
            rows = modulation[-1][block]
            if groups > 1:
                rows = jnp.repeat(rows, row_count // groups, axis=0)
            return [rows[:, k * features : (k + 1) * features] for k in range(6)]

        spatial_pieces, temporal_pieces = pieces_of(0), pieces_of(1)
        spatial_parts, temporal_parts = weights.fetch(spatial_shards, temporal_shards)
        same = (place_of[:, :, None] == place_of[:, None, :])[:, None, :, :]
        itself = lambda array: array
        spatial_batch = groups * own_frames
        spatial_mix = lambda rows: attend(rows, spatial_batch, None, head, share_frame)
        spatial_mix_back = lambda g, rows: attend_back(
            g, rows, spatial_batch, None, head, share_frame, share_frame_back
        )
        temporal_mix = lambda rows: attend(rows, groups, same, head, itself)
        temporal_mix_back = lambda g, rows: attend_back(
            g, rows, groups, same, head, itself, itself
        )
        spatial_in = to_frames(tokens).astype(FULL)
        spatial_out, spatial_saved = block_forward(
            spatial_in, spatial_pieces, spatial_parts, spatial_mix
        )
        temporal_in = to_patches(spatial_out.astype(LOW)).astype(FULL)
        result, temporal_saved = block_forward(
            temporal_in, temporal_pieces, temporal_parts, temporal_mix
        )
        out_tokens = result.astype(LOW).reshape(tokens.shape)
        incoming = cotangent.astype(FULL).reshape(row_count, features)
        grad_temporal_in, temporal_sums, temporal_grads = block_backward(
            incoming,
            temporal_pieces,
            temporal_parts,
            temporal_saved,
            temporal_mix_back,
            weights,
            groups,
            True,
        )
        grad_spatial_out = to_frames(grad_temporal_in.astype(LOW)).astype(FULL)
        grad_spatial_in, spatial_sums, spatial_grads = block_backward(
            grad_spatial_out,
            spatial_pieces,
            spatial_parts,
            spatial_saved,
            spatial_mix_back,
            weights,
            groups,
            False,
        )
        grad_tokens = to_patches(grad_spatial_in.astype(LOW)).astype(FULL).reshape(tokens.shape)
        condition_grads = conditions_at_once(spatial_sums, temporal_sums)

    grad_class_table, grad_mod_spatial, grad_mod_temporal = condition_grads

    return (
        out_tokens,
        grad_tokens,
        grad_class_table,
        grad_mod_spatial,
        *spatial_grads,
        grad_mod_temporal,
        *temporal_grads,
    )


def solution(mesh):
    patch, seq = mesh.shape["patch"], mesh.shape["seq"]
    patch_axes, seq_axis = "patch", "seq"
    if seq == 2 and patch % 4 == 0:
        patch_axes, seq_axis = ("z", "y", "core"), "x"
        mesh = Mesh(mesh.devices.reshape(patch // 4, 2, 2, seq), patch_axes + (seq_axis,))
    rows = P(seq_axis, None, patch_axes, None)
    both = P(patch_axes, seq_axis)
    return jax.shard_map(
        partial(per_device, patch, seq, patch_axes, seq_axis),
        mesh=mesh,
        in_specs=(rows, rows, P(seq_axis), P(seq_axis), P(seq_axis, None), P()) + (both,) * 10,
        out_specs=(rows, rows, P()) + (both,) * 10,
        check_vma=False,
    )
```

```python
import math
from functools import partial

import jax
import jax.numpy as jnp
from jax import lax
from jax.experimental import pallas as pl
from jax.experimental.pallas import tpu as pltpu
from jax.sharding import Mesh
from jax.sharding import PartitionSpec as P

HEADS = 16
EPSILON = 1e-06
PRECISE = lax.Precision.HIGHEST
LOW = jnp.bfloat16
FULL = jnp.float32


def time_features(step_ids, features):
    half_width = features // 2
    frequency = jnp.exp(-math.log(10000.0) * jnp.arange(half_width, dtype=FULL) / half_width)
    angles = step_ids.astype(FULL)[:, None] * frequency[None, :]
    return jnp.concatenate([jnp.cos(angles), jnp.sin(angles)], axis=-1)


def normalize(values):
    centred = values - jnp.mean(values, axis=-1, keepdims=True)
    inverse = lax.rsqrt(jnp.mean(centred * centred, axis=-1, keepdims=True) + EPSILON)
    return centred * inverse, inverse


def normalize_back(grad_norm, normed, inverse):
    return inverse * (
        grad_norm
        - jnp.mean(grad_norm, axis=-1, keepdims=True)
        - normed * jnp.mean(grad_norm * normed, axis=-1, keepdims=True)
    )


def matmul(left, right):
    return jnp.dot(left, right, preferred_element_type=FULL)


def matmul_nt(left, right):
    return lax.dot_general(left, right, (((1,), (1,)), ((), ())), preferred_element_type=FULL)


def matmul_tn(left, right):
    return lax.dot_general(left, right, (((0,), (0,)), ((), ())), preferred_element_type=FULL)


def in_order(pieces, first):
    count = len(pieces)
    return [lax.select_n((k - first) % count, *pieces) for k in range(count)]


def pick(array, axis, index):
    return lax.dynamic_index_in_dim(array, index, axis, keepdims=False)


LIMIT = 60 * 2**20
TINY = pl.CostEstimate(flops=1, bytes_accessed=1, transcendentals=0)
CHIPS_Y = 2


def at_rows(index, rows):
    return pl.ds(pl.multiple_of(index * rows, 16), rows)


class Weight:
    def __init__(self, depth, rows, cols, strips):
        self.depth, self.rows, self.cols, self.strips = depth, rows, cols, strips
        self.width = max(strip[6] + strip[7] for strip in strips)
        self.arrays = []
        for strip in strips:
            if not any(strip[0][0] is array for array in self.arrays):
                self.arrays += strip[0]

    def scratch(self):
        return [
            pltpu.VMEM((2, 2 * self.depth * self.rows, self.width), LOW),
            pltpu.SemaphoreType.DMA((2, 2, self.depth * len(self.strips))),
        ]

    def copies(self, where, refs, held, sems):
        found = []
        for side in range(2):
            group = []
            x = lax.rem(where[3] + side, 2)
            for turn in range(2):
                y = lax.rem(where[1] + turn, 2)
                for ahead in range(self.depth):
                    z = lax.rem(where[0] + ahead, self.depth)
                    at = (z * CHIPS_Y + y) * self.rows
                    for number, strip in enumerate(self.strips):
                        arrays, x_first, z_placed, source_lane, row, rows, lane, lanes = strip
                        base = [k for k, a in enumerate(self.arrays) if a is arrays[0]][0]
                        first, second = (side, turn) if x_first else (turn, side)
                        source = refs[base + second].at[
                            first,
                            z if z_placed else ahead,
                            :,
                            source_lane : source_lane + lanes,
                        ]
                        start = pl.multiple_of(at + row, 16)
                        target = held.at[x, pl.ds(start, rows), lane : lane + lanes]
                        sem = sems.at[side, turn, ahead * len(self.strips) + number]
                        group.append(pltpu.make_async_copy(source, target, sem))
            found.append(group)
        return found


def start_all(copies):
    for copy in copies:
        copy.start()


def wait_all(copies):
    for copy in copies:
        copy.wait()


def dot(left, right):
    return lax.dot_general(left, right, (((1,), (0,)), ((), ())), preferred_element_type=FULL)


def dot_nt(left, right):
    return lax.dot_general(left, right, (((1,), (1,)), ((), ())), preferred_element_type=FULL)


def dot_tn(left, right):
    return lax.dot_general(left, right, (((0,), (0,)), ((), ())), preferred_element_type=FULL)


def call(body, where, ins, outs, scratch, flops, name, after=()):
    count = len(ins)

    def kernel(where_ref, *refs):
        body(where_ref, *refs[:count], *refs[count + len(after) :])

    vmem = pl.BlockSpec(memory_space=pltpu.VMEM)
    hbm = pl.BlockSpec(memory_space=pl.ANY)
    size = sum(a.size * a.dtype.itemsize for a, _ in ins)
    size += sum(math.prod(o.shape) * o.dtype.itemsize for o in outs)
    return pl.pallas_call(
        kernel,
        out_shape=outs,
        in_specs=[pl.BlockSpec(memory_space=pltpu.SMEM)]
        + [vmem if inside else hbm for _, inside in ins]
        + [hbm] * len(after),
        out_specs=[vmem] * len(outs),
        scratch_shapes=scratch,
        compiler_params=pltpu.CompilerParams(vmem_limit_bytes=LIMIT),
        cost_estimate=TINY,
        name=name,
    )(where, *[a for a, _ in ins], *after)


def shape(dims, dtype):
    return jax.ShapeDtypeStruct(dims, dtype)


def by_place(first, pair):
    return [jnp.where(first, pair[0], pair[1]), jnp.where(first, pair[1], pair[0])]


def two_cores(refs):
    return jnp.concatenate([ref[...].astype(FULL) for ref in refs], axis=0)


def add_core(part, came):
    count = part.shape[0] // 2
    part, came = part[...].astype(FULL), came[...].astype(FULL)
    return jnp.concatenate([part[:count] + came[count:], part[count:] + came[:count]], axis=0)


def norm_qkv(where, rows, mods, weight, cols):
    count, features = rows[0].shape
    count *= 2
    many = len(weight.arrays)
    thin = weight.cols - cols
    chips = 2 * weight.depth
    part = weight.rows // 2

    def body(where, own, other, mods, *refs):
        sources, (hidden, out_weight, out, held, sems) = refs[:many], refs[many:]
        copies = weight.copies(where, sources, held, sems)
        for group in copies:
            start_all(group)
        normed, _ = normalize(two_cores((own, other)))
        value = (normed * (1.0 + mods[1:2]) + mods[0:1]).astype(LOW)
        hidden[0] = value
        for side in range(2):
            x = lax.rem(where[3] + side, 2)
            wait_all(copies[side])
            out[x] = dot(value, held[x, :, :cols]).astype(LOW)
            strips = held[x, :, cols:].astype(FULL).reshape(chips, 2, part, thin)
            both = [strips[:, k].reshape(chips * part, thin) for k in range(2)]
            out_weight[x] = jnp.concatenate(both, axis=1).astype(LOW)

    return call(
        body,
        where,
        [(a, True) for a in (*rows, mods)] + [(w, False) for w in weight.arrays],
        [
            shape((1, count, features), LOW),
            shape((2, chips * part, 2 * thin), LOW),
            shape((2, count, cols), LOW),
        ],
        weight.scratch(),
        4 * count * features * cols,
        "norm_qkv",
    )


def head_slices(qkv, rows, number, heads, head):
    def column(slot):
        per = 3 * heads // 2
        x, at = divmod(slot, per)
        return qkv[x, rows, at * head : (at + 1) * head]

    return column(number), column(heads + number), column(2 * heads + number)


def probabilities(query, key, mask, factor):
    scores = dot_nt(key, query) * factor
    if mask is not None:
        scores = jnp.where(mask, scores, -1e30)
    weights = jnp.exp(scores - jnp.max(scores, axis=0, keepdims=True))
    return weights * (1.0 / jnp.sum(weights, axis=0, keepdims=True))


def attend_out(where, qkv, out_weight, marks, head):
    _, count, cols = qkv.shape
    heads = 2 * cols // (3 * head)
    size = count // 2

    def body(where, qkv, out_weight, *refs):
        mask = None
        if marks is not None:
            mask = refs[0][...] == refs[1][...]
        attended, part = refs[-2:]
        for block in range(2):
            rows = slice(block * size, (block + 1) * size)
            mixed = []
            for number in range(heads):
                query, key, value = head_slices(qkv, rows, number, heads, head)
                probs = probabilities(query, key, mask, head ** (-0.5)).astype(LOW)
                mixed.append(dot_tn(value, probs))
            result = jnp.concatenate(mixed, axis=0).T.astype(LOW)
            attended[0, rows] = result
            sides = [dot(result, out_weight[x]) for x in range(2)]
            part[rows] = jnp.concatenate(sides, axis=1).astype(LOW)

    ins = [(qkv, True), (out_weight, True)] + ([] if marks is None else [(m, True) for m in marks])
    return call(
        body,
        where,
        ins,
        [shape((1, count, heads * head), LOW), shape((count, 2 * out_weight.shape[2]), LOW)],
        [],
        8 * heads * count * size * head,
        "attend_out",
    )


GELU_A = math.sqrt(2.0 / math.pi)
GELU_B = 0.044715


def gelu(value):
    inner = GELU_A * (value + GELU_B * value * value * value)
    return 0.5 * value * (1.0 + jnp.tanh(inner))


def gelu_slope(value):
    square = value * value
    bend = jnp.tanh(GELU_A * (value + GELU_B * square * value))
    return 0.5 * (1.0 + bend) + 0.5 * value * (1.0 - bend * bend) * GELU_A * (
        1.0 + 3.0 * GELU_B * square
    )


def norm_up(where, part, came, rows, mods, weight):
    count, features = part.shape
    cols, many = weight.cols, len(weight.arrays)

    def body(where, part, came, own, other, mods, *refs):
        sources, (branch, middle, hidden, pre, act, held, sems) = refs[:many], refs[many:]
        copies = weight.copies(where, sources, held, sems)
        for group in copies:
            start_all(group)
        value = add_core(part, came)
        branch[...] = value
        total = two_cores((own, other)) + mods[2:3] * value
        middle[...] = total
        normed, _ = normalize(total)
        value = (normed * (1.0 + mods[4:5]) + mods[3:4]).astype(LOW)
        hidden[0] = value
        for side in range(2):
            x = lax.rem(where[3] + side, 2)
            wait_all(copies[side])
            before = dot(value, held[x])
            pre[x] = before.astype(LOW)
            act[x] = gelu(before).astype(LOW)

    dims = (count, features)
    return call(
        body,
        where,
        [(a, True) for a in (part, came, *rows, mods)] + [(w, False) for w in weight.arrays],
        [shape(dims, FULL), shape(dims, FULL), shape((1,) + dims, LOW)]
        + [shape((2, count, cols), LOW)] * 2,
        weight.scratch(),
        4 * count * features * cols,
        "norm_up",
    )


def down_part(where, act, weight):
    _, count, wide = act.shape
    many = len(weight.arrays)

    def body(where, act, *refs):
        sources, (out, held, sems) = refs[:many], refs[many:]
        copies = weight.copies(where, sources, held, sems)
        for group in copies:
            start_all(group)
        totals = []
        for side in range(2):
            place = lax.rem(where[3] + side, 2)
            wait_all(copies[side])
            total = dot(act[0], held[place, :wide]) + dot(act[1], held[place, wide:])
            totals.append(total[:, : weight.cols].astype(LOW))
        out[...] = jnp.concatenate(by_place(where[3] == 0, totals), axis=1)

    return call(
        body,
        where,
        [(act, True)] + [(w, False) for w in weight.arrays],
        [shape((count, 2 * weight.cols), LOW)],
        weight.scratch(),
        8 * count * wide * weight.cols,
        "down_part",
    )[0]


def finish(where, part, came, middle, mods):
    count, features = part.shape

    def body(where, part, came, middle, mods, mlp, out):
        total = add_core(part, came)
        mlp[...] = total
        size = count // 2
        out[...] = (middle[:size] + mods[5:6] * total[:size]).astype(LOW)

    return call(
        body,
        where,
        [(a, True) for a in (part, came, middle, mods)],
        [shape((count, features), FULL), shape((count // 2, features), LOW)],
        [],
        0,
        "finish",
    )


def column_sums(*values):
    sums = [jnp.sum(v, axis=0, keepdims=True) for v in values]
    fill = jnp.zeros((8 - len(sums), sums[0].shape[1]), FULL)
    return jnp.concatenate(sums + [fill], axis=0)


def mlp_back(where, grads, mods, pre, up, down):
    count, features = grads[0].shape
    count *= 2
    wide = pre.shape[-1]
    cols = down.cols
    many_up, many_down = len(up.arrays), len(down.arrays)

    def body(where, own, other, mods, pre, *refs):
        ups, downs = refs[:many_up], refs[many_up : many_up + many_down]
        grad_mlp, grad_pre, part, up_held, up_sems, down_held, down_sems = refs[many_up + many_down :]
        down_copies = down.copies(where, downs, down_held, down_sems)
        up_copies = up.copies(where, ups, up_held, up_sems)
        for group in down_copies + up_copies:
            start_all(group)
        scaled = (mods[5:6] * two_cores((own, other))).astype(LOW)
        sides = [scaled[:, s * cols : (s + 1) * cols] for s in range(2)]
        for s in range(2):
            grad_mlp[s] = sides[s]
        wait_all(down_copies[0] + down_copies[1])
        total = None
        for side in range(2):
            x = lax.rem(where[3] + side, 2)
            rows = pl.ds(pl.multiple_of(x * wide, 16), wide)
            grad_act = dot_nt(sides[0], down_held[0, rows, :cols]) + dot_nt(
                sides[1], down_held[1, rows, :cols]
            )
            value = (gelu_slope(pre[x].astype(FULL)) * grad_act).astype(LOW)
            grad_pre[x] = value
            wait_all(up_copies[side])
            piece = dot_nt(value, up_held[x])
            total = piece if total is None else total + piece
        part[...] = total.astype(LOW)

    return call(
        body,
        where,
        [(a, True) for a in (*grads, mods, pre)] + [(w, False) for w in up.arrays + down.arrays],
        [
            shape((2, count, cols), LOW),
            shape((2, count, wide), LOW),
            shape((count, features), LOW),
        ],
        up.scratch() + down.scratch(),
        8 * count * features * wide,
        "mlp_back",
    )


def attend_grad(
    where, part, came, grads, mods, middle, branch, mlp, out_weight, qkv, marks, head
):
    _, count, cols = qkv.shape
    heads = 2 * cols // (3 * head)
    factor = head ** (-0.5)
    features = part.shape[1]
    wide = features // 2
    size = count // 2

    def body(where, part, came, own, other, mods, middle, branch, mlp, out_weight, qkv, *refs):
        mask = None
        if marks is not None:
            mask = refs[0][...] == refs[1][...]
        grad_mid, grad_branch, sums, out = refs[-4:]
        incoming = two_cores((own, other))
        total = add_core(part, came)
        normed, inverse = normalize(middle[...])
        result = incoming + normalize_back(total * (1.0 + mods[4:5]), normed, inverse)
        grad_mid[...] = result
        sums[...] = column_sums(result * branch[...], total, total * normed, incoming * mlp[...])
        scaled = (mods[2:3] * result).astype(LOW)
        sides = [scaled[:, s * wide : (s + 1) * wide] for s in range(2)]
        for s in range(2):
            grad_branch[s] = sides[s]
        attended = dot_nt(sides[0], out_weight[0]) + dot_nt(sides[1], out_weight[1])
        attended = attended.astype(LOW)
        for block in range(2):
            rows = slice(block * size, (block + 1) * size)
            pieces = [None] * (3 * heads)
            for number in range(heads):
                grad = attended[rows, number * head : (number + 1) * head]
                query, key, value = head_slices(qkv, rows, number, heads, head)
                probs = probabilities(query, key, mask, factor)
                grad_probs = dot_nt(value, grad)
                delta = jnp.sum(grad_probs * probs, axis=0, keepdims=True)
                grad_scores = (probs * (grad_probs - delta)).astype(LOW)
                pieces[number] = (dot_tn(key, grad_scores).T * factor).astype(LOW)
                pieces[heads + number] = (dot(grad_scores, query) * factor).astype(LOW)
                pieces[2 * heads + number] = dot(probs.astype(LOW), grad).astype(LOW)
            per = 3 * heads // 2
            for x in range(2):
                out[x, rows] = jnp.concatenate(pieces[x * per : (x + 1) * per], axis=1)

    ins = [(a, True) for a in (part, came, *grads, mods, middle, branch, mlp, out_weight, qkv)]
    ins += [] if marks is None else [(m, True) for m in marks]
    return call(
        body,
        where,
        ins,
        [
            shape((count, features), FULL),
            shape((2, count, wide), LOW),
            shape((8, features), FULL),
            shape((2, count, cols), LOW),
        ],
        [],
        20 * heads * count * size * head,
        "attend_grad",
    )


def qkv_part(where, grad_qkv, weight, features):
    _, count, cols = grad_qkv.shape
    many = len(weight.arrays)

    def body(where, grad_qkv, *refs):
        sources, (out, held, sems) = refs[:many], refs[many:]
        copies = weight.copies(where, sources, held, sems)
        for group in copies:
            start_all(group)
        total = None
        for side in range(2):
            x = lax.rem(where[3] + side, 2)
            wait_all(copies[side])
            piece = dot_nt(grad_qkv[x], held[x, :, :cols])
            total = piece if total is None else total + piece
        out[...] = total.astype(LOW)

    return call(
        body,
        where,
        [(grad_qkv, True)] + [(w, False) for w in weight.arrays],
        [shape((count, features), LOW)],
        weight.scratch(),
        4 * count * features * cols,
        "qkv_part",
    )[0]


def finish_back(where, part, came, rows, mods, grad_mid):
    count, features = part.shape

    def body(where, part, came, own, other, mods, grad_mid, out, sums):
        total = add_core(part, came)
        normed, inverse = normalize(two_cores((own, other)))
        back = normalize_back(total * (1.0 + mods[1:2]), normed, inverse)
        sums[...] = column_sums(total, total * normed)
        size = count // 2
        out[...] = (grad_mid[:size] + back[:size]).astype(LOW)

    return call(
        body,
        where,
        [(a, True) for a in (part, came, *rows, mods, grad_mid)],
        [shape((count // 2, features), LOW), shape((8, features), FULL)],
        [],
        0,
        "finish_back",
    )


def weight_grad(where, left, right, tail, depth, cut):
    blocks, count, wide = left.shape
    rows = blocks * wide // (2 * depth)
    cols = right.shape[-1]
    operands = [left, right]
    scratch = [pltpu.VMEM((blocks * wide, count), LOW)]
    if tail is not None:
        size, thin = tail[0].shape[-1], tail[1].shape[-1] // 2
        operands += tail
        scratch.append(pltpu.VMEM((size, count), LOW))
        cols += thin
    many = len(operands)
    cuts = [(at, to) for at, to in ((0, cut), (cut, cols)) if to > at]

    def kernel(where, *refs):
        ins, outs, held = refs[:many], refs[many : -len(scratch)], refs[-len(scratch) :]
        z = pl.program_id(0)

        @pl.when(z == 0)
        def _():
            for source, flipped in zip(ins[::2], held):
                size = source.shape[-1]
                for block in range(source.shape[0]):
                    flipped[block * size : (block + 1) * size] = source[block].T

        chosen = []
        for flipped in held:
            size = flipped.shape[0] // depth
            chosen.append(flipped[pl.ds(pl.multiple_of(z * size, 16), size)])

        for turn, x in enumerate((1 - where[3], where[3])):
            value = dot(chosen[0], ins[1][x])
            value = [value[:rows], value[rows:]]
            if tail is not None:
                more = dot(chosen[1], ins[3][x])
                size = more.shape[0] // 2
                for y in range(2):
                    part = more[y * size : (y + 1) * size]
                    strips = jnp.concatenate([part[:, :thin], part[:, thin:]], axis=0)
                    value[y] = jnp.concatenate([value[y], strips], axis=1)
            own, other = by_place(where[1] == 0, value)
            for number, (at, to) in enumerate(cuts):
                outs[4 * number + 2 * turn][0] = other[:, at:to].astype(LOW)
                outs[4 * number + 2 * turn + 1][0] = own[:, at:to].astype(LOW)

    def whole(a):
        return pl.BlockSpec(a.shape, lambda i, s: (0,) * len(a.shape))

    widths = [to - at for at, to in cuts for _ in range(4)]
    return pl.pallas_call(
        kernel,
        out_shape=[shape((depth, rows, w), LOW) for w in widths],
        grid_spec=pltpu.PrefetchScalarGridSpec(
            num_scalar_prefetch=1,
            grid=(depth,),
            in_specs=[whole(a) for a in operands],
            out_specs=[pl.BlockSpec((1, rows, w), lambda i, s: (i, 0, 0)) for w in widths],
            scratch_shapes=scratch,
        ),
        compiler_params=pltpu.CompilerParams(vmem_limit_bytes=LIMIT),
        cost_estimate=TINY,
        name="weight_grad",
    )(where, *operands)


def add_all(where, *arrays):
    depth, rows, cols = arrays[0].shape

    def kernel(where, *refs):
        total = refs[0][...].astype(FULL)
        for ref in refs[1:-1]:
            total = total + ref[...].astype(FULL)
        refs[-1][...] = total.astype(LOW)

    moving = pl.BlockSpec((1, rows, cols), lambda i, s: (i, 0, 0))
    return pl.pallas_call(
        kernel,
        out_shape=shape((depth, rows, cols), LOW),
        grid_spec=pltpu.PrefetchScalarGridSpec(
            num_scalar_prefetch=1,
            grid=(depth,),
            in_specs=[moving] * len(arrays),
            out_specs=moving,
        ),
        compiler_params=pltpu.CompilerParams(vmem_limit_bytes=LIMIT),
        cost_estimate=TINY,
        name="add_all",
    )(where, *arrays)


def add_planes(where, *strips):
    depth, rows, _ = strips[0][0].shape
    count = len(strips[0])
    cols = sum(a.shape[-1] for a in strips[0])

    def body(where, *refs):
        ins, outs = refs[: count * len(strips)], refs[count * len(strips) :]
        for ahead, out in enumerate(outs):
            z = lax.rem(where[0] + ahead, depth)
            at = 0
            for number in range(count):
                total = ins[number][z].astype(FULL)
                for ref in ins[number + count :: count]:
                    total = total + ref[z].astype(FULL)
                wide = total.shape[-1]
                out[:, at : at + wide] = total.astype(out.dtype)
                at += wide

    return call(
        body,
        where,
        [(a, True) for group in strips for a in group],
        [shape((rows, cols), FULL)] + [shape((rows, cols), LOW)] * (depth - 1),
        [],
        0,
        "add_planes",
    )


def add_planes_last(where, *planes):
    def body(where, *refs):
        total = refs[0][...]
        for ref in refs[1:-1]:
            total = total + ref[...].astype(FULL)
        refs[-1][...] = total

    outs = [shape(planes[0].shape, FULL)]
    return call(body, where, [(p, True) for p in planes], outs, [], 0, "add_planes_last")[0]


def part_rows(where, totals, cols):
    rows = totals[0].shape[0]
    wide = sum(t.shape[1] for t in totals)
    part, thin = rows // 2, wide - cols

    def body(where, *refs):
        ins, outs = refs[: len(totals)], refs[len(totals) :]
        total = jnp.concatenate([ref[...].astype(FULL) for ref in ins], axis=1)
        mine, theirs = by_place(where[2] == 0, [total[:part, :cols], total[part:, :cols]])
        if thin:
            outs[0][...] = jnp.concatenate([total[:part, cols:], total[part:, cols:]], axis=1)
        outs[-2][...] = mine
        outs[-1][...] = theirs.astype(LOW)

    outs = [shape((part, cols), FULL), shape((part, cols), LOW)]
    if thin:
        outs.insert(0, shape((part, 2 * thin), FULL))
    return call(body, where, [(t, True) for t in totals], outs, [], 0, "part_rows")


def interleave(where, mine, theirs, width):
    rows, cols = mine.shape

    def body(where, mine, theirs, out):
        both = by_place(where[2] == 0, [mine[...], theirs[...].astype(FULL)])
        groups = []
        for at in range(0, cols, width):
            groups += [b[:, at : at + width] for b in both]
        out[...] = jnp.concatenate(groups, axis=1)

    return call(
        body,
        where,
        [(mine, True), (theirs, True)],
        [shape((rows, 2 * cols), FULL)],
        [],
        0,
        "interleave",
    )[0]


def deal(where, shards, widths):
    rows = shards[0].shape[0]
    cols = sum(a.shape[1] for a in shards) // 2

    def body(where, *refs):
        own, other = refs[-2:]
        halves = [[], []]
        for ref, width in zip(refs, widths):
            value = ref[...]
            for number in range(value.shape[1] // width):
                halves[number % 2].append(value[:, number * width : (number + 1) * width])
        pair = [jnp.concatenate(h, axis=1) for h in halves]
        own[...], other[...] = by_place(where[2] == 0, pair)

    return call(
        body,
        where,
        [(a, True) for a in shards],
        [shape((rows, cols), LOW)] * 2,
        [],
        0,
        "deal",
    )


def pack(where, own, got, outs, downs, cols):
    part = own.shape[0]
    rows = 2 * part
    thin = outs[0].shape[1] // 2
    wide = downs[0].shape[1]
    padded = -(-wide // 128) * 128
    count = downs[0].shape[0] // rows
    first = cols[0] + thin

    def body(where, own, got, out_s, out_t, down_s, down_t, qkv_s, mlp_s, packed):
        pair = by_place(where[2] == 0, [own[...].astype(FULL), got[...].astype(FULL)])
        both = jnp.concatenate(pair, axis=0)

        def strips(ref):
            value = ref[...].astype(FULL)
            return jnp.concatenate([value[:, :thin], value[:, thin:]], axis=0)

        def put_down(to, lane, down):
            for k in range(count):
                to[:, lane : lane + wide] = down[k * rows : (k + 1) * rows]
                if padded > wide:
                    to[:, lane + wide : lane + padded] = jnp.zeros((rows, padded - wide), LOW)
                lane += padded

        at = cols[0] + cols[1]
        qkv_s[...] = jnp.concatenate([both[:, : cols[0]], strips(out_s)], axis=1).astype(LOW)
        mlp_s[:, : cols[1]] = both[:, cols[0] : at].astype(LOW)
        put_down(mlp_s, cols[1], down_s)
        qkv_t = jnp.concatenate([both[:, at : at + cols[0]], strips(out_t)], axis=1)
        packed[:, :first] = qkv_t.astype(LOW)
        packed[:, first : first + cols[1]] = both[:, at + cols[0] :].astype(LOW)
        put_down(packed, first + cols[1], down_t)

    mlp = cols[1] + count * padded
    return call(
        body,
        where,
        [(a, True) for a in (own, got, *outs, *downs)],
        [shape((rows, first), LOW), shape((rows, mlp), LOW), shape((rows, first + mlp), LOW)],
        [],
        0,
        "pack",
    )


class Grid:
    def __init__(self, patch, seq, patch_axes, seq_axis):
        self.patch_axes, self.seq_axis = patch_axes, seq_axis
        self.every = (patch_axes if isinstance(patch_axes, tuple) else (patch_axes,)) + (seq_axis,)
        self.chips = self.every[:2] + (seq_axis,)
        self.patch, self.seq = patch, seq
        self.depth = patch // 4
        where = lax.axis_index(patch_axes)
        self.place = where
        self.core = where % 2
        self.y = (where // 2) % 2
        self.z = where // 4
        self.x = lax.axis_index(seq_axis)

    def moves(self, step):
        pairs = []
        for p in range(self.patch):
            for x in range(self.seq):
                z, y, c = p // 4, (p // 2) % 2, p % 2
                z2, y2, c2, x2 = step(z, y, c, x)
                pairs.append((p * self.seq + x, ((z2 * 2 + y2) * 2 + c2) * self.seq + x2))
        return pairs

    def send(self, array, step):
        return lax.ppermute(array, self.every, self.moves(step))

    def flip_core(self, array):
        return self.send(array, lambda z, y, c, x: (z, y, 1 - c, x))

    def flip_y(self, array):
        return self.send(array, lambda z, y, c, x: (z, 1 - y, c, x))

    def shift_x(self, array, by):
        return self.send(array, lambda z, y, c, x: (z, y, c, (x + by) % self.seq))

    def shift_z(self, array, by):
        return self.send(array, lambda z, y, c, x: ((z + by) % self.depth, y, c, x))

    def xor_patch(self, array, bit):
        pairs = [
            (p * self.seq + x, (p ^ bit) * self.seq + x)
            for p in range(self.patch)
            for x in range(self.seq)
        ]
        return lax.ppermute(array, self.every, pairs)

    def bits(self):
        bit = self.patch // 2
        while bit:
            yield bit
            bit //= 2

    def sum_patch(self, array):
        for bit in self.bits():
            array = array + self.xor_patch(array, bit)
        return array

    def join_patch(self, array, other, bit):
        mine_first = (self.place // bit) % 2 == 0
        return jnp.where(
            mine_first, jnp.concatenate([array, other]), jnp.concatenate([other, array])
        )

    def all_seq(self, array):
        return [array] + [self.shift_x(array, -j) for j in range(1, self.seq)]


class Flight:
    pass


class Split:
    def __init__(self, grid, head, group, token):
        self.grid = grid
        self.head, self.group = head, group
        self.up_cols = group * grid.patch // 4
        self.split_cut = 5 * 128
        self.token = token
        self.strict = True
        self.flights = []
        self.strict = True
        self.where = jnp.stack([grid.z, grid.y, grid.core, grid.x]).astype(jnp.int32)

    @staticmethod
    def fits(patch, seq, frames, features, hidden):
        return (
            patch == HEADS
            and patch == frames
            and seq == 2
            and features % (2 * patch) == 0
            and hidden % patch == 0
            and (2 * features // patch) % 16 == 0
            and hidden == 2 * 2 * features
            and (hidden // patch) % 32 == 0
        )


    def tie(self, *arrays):
        *arrays, self.token = lax.optimization_barrier((*arrays, self.token))
        return arrays[0] if len(arrays) == 1 else arrays

    def run(self, kernel, first, *rest):
        if isinstance(first, (list, tuple)):
            head, *tail = first
            if isinstance(head, tuple):
                first = [(self.tie(head[0]), *head[1:]), *tail]
            else:
                first = [self.tie(head), *tail]
        else:
            first = self.tie(first)
        result = kernel(self.where, first, *rest)
        if not self.strict:
            self.token = result[-1] if isinstance(result, (list, tuple)) else result
            return result
        if isinstance(result, (list, tuple)):
            return self.tie(*result) if len(result) > 1 else [self.tie(result[0])]
        return self.tie(result)

    def first(self, array, x_first):
        return self.grid.shift_x(array, 1) if x_first else self.grid.flip_y(array)

    def prepare(self, spatial, temporal):
        own, other = deal(
            self.where,
            [spatial[0], spatial[2], temporal[0], temporal[2]],
            [self.head, self.group] * 2,
        )
        got = self.grid.flip_core(other)
        cols = (spatial[0].shape[1] // 2, spatial[2].shape[1] // 2)
        outs, downs = [spatial[1], temporal[1]], [spatial[3], temporal[3]]
        return self.run(pack, own, got, outs, downs, cols)

    def gather_z(self, piece):
        piece = self.tie(piece)
        moves = [partial(self.grid.shift_z, by=-j) for j in range(1, self.grid.depth)]
        return piece, [self.fly(piece, move) for move in moves]

    def fly(self, array, move):
        flight = Flight()
        flight.value = move(self.tie(array))
        self.flights.append(flight)
        return flight

    def land(self, *chosen):
        chosen = chosen or tuple(self.flights)
        arrived = self.tie(*[flight.value for flight in chosen], self.token)
        for flight, value in zip(chosen, arrived):
            flight.value = value
        self.flights = [f for f in self.flights if not any(f is c for c in chosen)]

    def move_first(self, x_first):
        return partial(self.first, x_first=x_first)

    def split_rows(self, totals, cols, width):
        *rest, mine, theirs = self.run(part_rows, totals, cols)
        flight = self.fly(theirs, self.grid.flip_core)
        yield
        yield [self.run(interleave, mine, flight.value, width)] + rest

    def across_z(self, array):
        return lax.psum_scatter(array, self.grid.chips[0], scatter_dimension=0, tiled=False)

    def both(self, array):
        return [array, self.grid.flip_core(array)]

    def forward(self, rows, mods, mod_steps, shards, down_shape, marks, to_frames, to_patches):
        grid, head = self.grid, self.head
        qkv_s, mlp_s, packed = shards
        depth, count = grid.depth, qkv_s.shape[0]
        cols = qkv_s.shape[1], self.up_cols
        padded = (mlp_s.shape[1] - cols[1]) * count // down_shape[0]
        cut = self.split_cut
        chunk = 3 * head * HEADS // 4

        def halved(strips, width, placed):
            return [
                (strip.buffers, strip.x_first, placed, 0, 0, count, lane, lanes)
                for strip, lane, lanes in zip(strips, (0, cut), (cut, width - cut))
            ]

        def stacked(pieces, cuts):
            own, flights = pieces
            self.land(*flights)
            pieces = [own] + [flight.value for flight in flights]
            parts = [jnp.stack([p[:, at:to] for p in pieces]) for at, to in zip(cuts, cuts[1:])]
            parts = self.tie(*parts)
            return [Arriving(self, part, k % 2 == 0) for k, part in enumerate(parts)]

        pieces = self.gather_z(qkv_s)
        list(mod_steps)
        mods = mods()
        one = stacked(pieces, [0, cut, cols[0]])
        for strip in one:
            strip.first()
        rows = self.both(rows)
        pieces = self.gather_z(mlp_s)
        for strip in one:
            strip.second()
        self.land(*[strip.flight for strip in one])
        two = up, down = stacked(pieces, [0, cols[1], mlp_s.shape[1]])
        held_t = lax.all_gather(self.tie(packed), grid.chips[0], axis=0)
        for strip in two:
            strip.first()
        qkv_w = Weight(depth, count, cols[0], halved(one, cols[0], False))
        hidden_one, out_w, qkv = self.run(norm_qkv, rows, mods[0], qkv_w, chunk)
        attended, part = self.run(attend_out, qkv, out_w, None, head)
        came = self.fly(part, grid.flip_core)
        for strip in two:
            strip.second()
        self.land(came)
        held_t = self.tie(held_t)
        cuts = [0, cols[0], cols[0] + cols[1]]
        cuts += [cuts[-1] + padded, cuts[-1] + 2 * padded]
        strips = [self.tie(held_t[..., at:to]) for at, to in zip(cuts, cuts[1:])]
        strips = [Arriving(self, s, k % 2 == 0) for k, s in enumerate(strips)]
        for strip in strips[:2]:
            strip.first()
        self.land(*[strip.flight for strip in two])
        up_w = Weight(
            depth, count, cols[1], [(up.buffers, True, False, 0, 0, count, 0, cols[1])]
        )
        down_w = Weight(
            depth,
            *down_shape,
            [
                (down.buffers, False, False, k * padded, k * count, count, 0, padded)
                for k in range(down_shape[0] // count)
            ],
        )
        branch, middle, hidden_two, pre, act = self.run(
            norm_up, part, came.value, rows, mods[0], up_w
        )
        part = self.run(down_part, act, down_w)
        came = self.fly(part, grid.flip_core)
        for strip in strips[:2]:
            strip.second()
        for strip in strips[2:]:
            strip.first()
        self.land(came)
        mlp, result = self.run(finish, part, came.value, middle, mods[0])
        spatial = (
            (mods[0], None, rows),
            (qkv_w, out_w, up_w, down_w),
            (hidden_one, qkv, attended, branch, middle, hidden_two, pre, act, mlp),
        )

        for strip in strips[2:]:
            strip.second()
        moved = self.fly(result, to_patches)
        self.land(moved)
        rows = [moved.value, self.fly(moved.value, grid.flip_core)]
        self.land(rows[1])
        rows[1] = rows[1].value
        self.land(*[strip.flight for strip in strips[:2]])
        early, late = strips[:2]
        qkv_w = Weight(
            depth, count, cols[0], [(early.buffers, True, True, 0, 0, count, 0, cols[0])]
        )
        up_w = Weight(
            depth, count, cols[1], [(late.buffers, False, True, 0, 0, count, 0, cols[1])]
        )
        hidden_one, out_w, qkv = self.run(norm_qkv, rows, mods[1], qkv_w, chunk)
        attended, part = self.run(attend_out, qkv, out_w, marks, head)
        came = self.fly(part, grid.flip_core)
        self.land(came)
        branch, middle, hidden_two, pre, act = self.run(
            norm_up, part, came.value, rows, mods[1], up_w
        )
        self.land()
        down_w = Weight(
            depth,
            *down_shape,
            [
                (strip.buffers, strip.x_first, True, 0, k * count, count, 0, padded)
                for k, strip in enumerate(strips[2:])
            ],
        )
        part = self.run(down_part, act, down_w)
        came = self.fly(part, grid.flip_core)
        self.land()
        mlp, result = self.run(finish, part, came.value, middle, mods[1])
        temporal = (
            (mods[1], marks, rows),
            (qkv_w, out_w, up_w, down_w),
            (hidden_one, qkv, attended, branch, middle, hidden_two, pre, act, mlp),
        )
        return result, spatial, temporal

    def grads_of(self, left, right, tail, cut, orders):
        quads = self.run(weight_grad, left, right, tail, self.grid.depth, cut)
        return [Strip(self, quads[4 * k : 4 * k + 4], order) for k, order in enumerate(orders)]

    def backward(self, spatial, temporal, grad, move, move_back, condition_steps):
        start = self.token
        self.strict = False
        head, flip = self.head, self.grid.flip_core
        (mods, marks, rows), (qkv_w, out_w, up_w, down_w), saved = temporal
        hidden_one, qkv, attended, branch, middle, hidden_two, pre, act, mlp = saved
        features = grad.shape[-1]
        wide, half = 2 * features // 2, features // 2
        chunk = 3 * half // 2
        grads = self.both(grad)
        grad_mlp, grad_pre, part = self.run(mlp_back, grads, mods, pre, up_w, down_w)
        came = self.fly(part, flip)
        (up_t,) = self.grads_of(hidden_two, grad_pre, None, wide, [True])
        self.land()

        up_t.first(0)
        (down_t,) = self.grads_of(act, grad_mlp, None, 0, [False])
        grad_mid, grad_branch, sums_two, grad_qkv = self.run(
            attend_grad,
            part,
            came.value,
            grads,
            mods,
            middle,
            branch,
            mlp,
            out_w,
            qkv,
            marks,
            head,
        )
        self.land()

        up_t.first(1)
        down_t.first(0)
        part = self.run(qkv_part, grad_qkv, qkv_w, features)
        came = self.fly(part, flip)
        (qkv_t,) = self.grads_of(hidden_one, grad_qkv, [attended, grad_branch], wide, [True])
        self.land()

        down_t.first(1)
        grad, sums_one = self.run(finish_back, part, came.value, rows, mods, grad_mid)
        mods_t = jnp.concatenate([sums_one[:2], sums_two[:4]], axis=0).reshape(1, -1)
        moved = self.fly(grad, move)
        up_t.second()
        self.land()

        qkv_t.first(0)
        grads = [moved.value, self.fly(moved.value, flip)]
        down_t.add_second()
        self.land()
        grads[1] = grads[1].value

        qkv_t.first(1)
        up_t.fly_second()
        (mods, marks, rows), (qkv_w, out_w, up_w, down_w), saved = spatial
        hidden_one, qkv, attended, branch, middle, hidden_two, pre, act, mlp = saved
        grad_mlp, grad_pre, part = self.run(mlp_back, grads, mods, pre, up_w, down_w)
        self.land()

        came = self.fly(part, flip)
        down_t.fly_second()
        (up_s,) = self.grads_of(hidden_two, grad_pre, None, wide, [False])
        (down_s,) = self.grads_of(act, grad_mlp, None, half, [True])
        up_t.total()
        self.land()

        up_s.first(0)
        down_s.first(0)
        up_z = self.across_z(up_t.sum)
        down_t.total()
        down_z = self.across_z(down_t.sum)
        grad_mid, grad_branch, sums_two, grad_qkv = self.run(
            attend_grad,
            part,
            came.value,
            grads,
            mods,
            middle,
            branch,
            mlp,
            out_w,
            qkv,
            marks,
            head,
        )
        qkv_t.add_second()
        self.land()

        up_s.first(1)
        down_s.first(1)
        (early, late) = self.grads_of(
            hidden_one, grad_qkv, [attended, grad_branch], self.split_cut, [True, False]
        )
        part = self.run(qkv_part, grad_qkv, qkv_w, features)
        came = self.fly(part, flip)
        self.land()

        early.first(0)
        late.first(0)
        qkv_t.fly_second()
        grad, sums_one = self.run(finish_back, part, came.value, rows, mods, grad_mid)
        mods_s = jnp.concatenate([sums_one[:2], sums_two[:4]], axis=0).reshape(1, -1)
        up_s.add_second()
        down_s.add_second()
        self.land()

        early.first(1)
        late.first(1)
        up_s.fly_second()
        down_s.fly_second()
        chain = Chain(self, condition_steps(mods_s, mods_t))
        qkv_t.total()
        qkv_z = self.across_z(qkv_t.sum)
        early.add_second()
        late.add_second()
        self.land()

        early.fly_second()
        late.fly_second()
        up_s.total()
        up_sz = self.across_z(up_s.sum)
        down_s.total()
        down_sz = self.across_z(down_s.sum)
        self.land()
        self.strict = True
        self.token, _ = lax.optimization_barrier((start, self.token))
        own, *planes = self.run(
            add_planes,
            [early.near[1], late.near[1]],
            [early.came[1].value, late.came[1].value],
            [early.last.value, late.last.value],
        )
        planes = [
            self.fly(plane, partial(self.grid.shift_z, by=j + 1)) for j, plane in enumerate(planes)
        ]
        for _ in range(4):
            chain.advance()
        up_t = self.split_rows([up_z], wide, self.group)
        next(up_t)
        self.land(self.flights[-1])
        (up_t,) = next(up_t)
        chain.advance()
        qkv_t = self.split_rows([qkv_z], chunk, head)
        next(qkv_t)
        self.land(self.flights[-1])
        qkv_t, out_t = next(qkv_t)
        chain.advance()
        tokens = self.fly(grad, move_back)
        chain.advance()
        self.land(*planes)
        qkv_sz = self.run(add_planes_last, own, *[plane.value for plane in planes])
        qkv_s = self.split_rows([qkv_sz], chunk, head)
        next(qkv_s)
        chain.advance()
        up_s = self.split_rows([up_sz], wide, self.group)
        next(up_s)
        chain.advance()
        self.land()
        qkv_s, out_s = next(qkv_s)
        (up_s,) = next(up_s)
        down_t, down_s = down_z.astype(FULL), down_sz.astype(FULL)
        grads = (qkv_s, out_s, up_s, down_s), (qkv_t, out_t, up_t, down_t)
        return tokens.value, chain.result, *grads


class Chain:
    def __init__(self, plan, steps):
        self.plan, self.steps = plan, steps
        self.flight = plan.fly(*next(steps))

    def advance(self):
        self.plan.land(self.flight)
        request = self.steps.send(self.flight.value)
        if isinstance(request[1], partial):
            self.flight = self.plan.fly(*request)
        else:
            self.result = request


class Arriving:
    def __init__(self, plan, held, x_first):
        self.plan, self.held, self.x_first = plan, held, x_first

    def first(self):
        self.flight = self.plan.fly(self.held, self.plan.move_first(self.x_first))

    def second(self):
        self.plan.land(self.flight)
        self.held = self.plan.tie(jnp.stack([self.held, self.flight.value]))
        self.flight = self.plan.fly(self.held, self.plan.move_first(not self.x_first))

    @property
    def buffers(self):
        return [self.held, self.flight.value]


class Strip:
    def __init__(self, plan, quads, x_first):
        self.plan, self.x_first = plan, x_first
        far = [quads[0], quads[1] if x_first else quads[2]]
        self.near = [quads[2] if x_first else quads[1], quads[3]]
        self.far, self.came = far, [None, None]

    def first(self, turn):
        self.came[turn] = self.plan.fly(self.far[turn], self.plan.move_first(self.x_first))

    def add_second(self):
        self.send = self.plan.run(add_all, self.near[0], self.came[0].value)

    def fly_second(self):
        self.last = self.plan.fly(self.send, self.plan.move_first(not self.x_first))

    def second(self):
        self.add_second()

    def total(self):
        self.sum = self.plan.run(add_all, self.near[1], self.came[1].value, self.last.value)


class WholeWeights:
    def __init__(self, grid, features, hidden):
        self.features, self.hidden = features, hidden

    def gather(self, local):
        wide = lax.all_gather(local, "seq", axis=1, tiled=True)
        return lax.all_gather(wide, "patch", axis=0, tiled=True)

    def fetch(self, spatial, temporal):
        return [[tuple(self.gather(w) for w in block)] for block in (spatial, temporal)]

    def scatter(self, grad):
        rows = lax.psum_scatter(grad.astype(LOW), "patch", scatter_dimension=0, tiled=True)
        return lax.psum_scatter(rows, "seq", scatter_dimension=1, tiled=True).astype(FULL)

    def reduce_mlp(self, hidden, grad_pre, activated, grad_mlp, flip):
        return (
            self.scatter(matmul_tn(hidden, grad_pre[0])),
            self.scatter(matmul_tn(activated[0], grad_mlp)),
        )

    def reduce_out(self, attended, grad_branch, flip):
        return self.scatter(matmul_tn(attended[0], grad_branch))

    def reduce_qkv(self, hidden, grad_qkv, flip):
        return self.scatter(matmul_tn(hidden, grad_qkv[0]))


def attention(queries, keys, mask, factor):
    scores = jnp.einsum("bphd,bkhd->bhpk", queries, keys, preferred_element_type=FULL) * factor
    if mask is not None:
        scores = jnp.where(mask, scores, -1e30)
    top = jnp.max(scores, axis=-1, keepdims=True)
    weights = jnp.exp(scores - top)
    return weights / jnp.sum(weights, axis=-1, keepdims=True)


def attend(qkv, batch, mask, head, share):
    rows = qkv.reshape(batch, -1, 3, qkv.shape[-1] // (3 * head), head)
    keys, values = share(rows[:, :, 1]), share(rows[:, :, 2])
    probs = attention(rows[:, :, 0], keys, mask, head ** (-0.5)).astype(LOW)
    mixed = jnp.einsum("bhpk,bkhd->bphd", probs, values, preferred_element_type=FULL)
    return mixed.reshape(qkv.shape[0], -1).astype(LOW)


def attend_back(grad, qkv, batch, mask, head, share, share_back):
    factor = head ** (-0.5)
    heads = qkv.shape[-1] // (3 * head)
    rows = qkv.reshape(batch, -1, 3, heads, head)
    grad_rows = grad.reshape(batch, -1, heads, head)
    queries, keys, values = rows[:, :, 0], share(rows[:, :, 1]), share(rows[:, :, 2])
    probs = attention(queries, keys, mask, factor)
    grad_probs = jnp.einsum("bphd,bkhd->bhpk", grad_rows, values, preferred_element_type=FULL)
    delta = jnp.sum(grad_probs * probs, axis=-1, keepdims=True)
    grad_scores = (probs * (grad_probs - delta)).astype(LOW)
    grad_queries = (
        jnp.einsum("bhpk,bkhd->bphd", grad_scores, keys, preferred_element_type=FULL) * factor
    )
    grad_keys = (
        jnp.einsum("bhpk,bphd->bkhd", grad_scores, queries, preferred_element_type=FULL) * factor
    )
    grad_values = jnp.einsum(
        "bhpk,bphd->bkhd", probs.astype(LOW), grad_rows, preferred_element_type=FULL
    )
    joined = jnp.stack(
        [grad_queries, share_back(grad_keys), share_back(grad_values)], axis=2
    )
    return joined.reshape(qkv.shape[0], -1).astype(LOW)


def total_parts(parts):
    total = parts[0]
    for part in parts[1:]:
        total = total + part
    return total


def block_forward(residual, pieces, parts, mix):
    normed_one, inverse_one = normalize(residual)
    hidden_one = (normed_one * (1.0 + pieces[1]) + pieces[0]).astype(LOW)
    qkv = [matmul(hidden_one, part[0]).astype(LOW) for part in parts]
    attended = [mix(rows) for rows in qkv]
    branch = total_parts([matmul(a, part[1]) for a, part in zip(attended, parts)])
    middle = residual + pieces[2] * branch
    normed_two, inverse_two = normalize(middle)
    hidden_two = (normed_two * (1.0 + pieces[4]) + pieces[3]).astype(LOW)
    pre = [matmul(hidden_two, part[2]) for part in parts]
    activated = [jax.nn.gelu(v, approximate=True).astype(LOW) for v in pre]
    mlp = total_parts([matmul(a, part[3]) for a, part in zip(activated, parts)])
    result = middle + pieces[5] * mlp
    saved = (
        normed_one,
        inverse_one,
        hidden_one,
        qkv,
        attended,
        branch,
        normed_two,
        inverse_two,
        hidden_two,
        pre,
        activated,
        mlp,
    )
    return result, saved


def block_backward(incoming, pieces, parts, saved, mix_back, weights, groups, flip):
    (
        normed_one,
        inverse_one,
        hidden_one,
        qkv,
        attended,
        branch,
        normed_two,
        inverse_two,
        hidden_two,
        pre,
        activated,
        mlp,
    ) = saved
    grad_mlp = (pieces[5] * incoming).astype(LOW)
    grad_pre = []
    for part, v in zip(parts, pre):
        _, back = jax.vjp(partial(jax.nn.gelu, approximate=True), v)
        grad_pre.append(back(matmul_nt(grad_mlp, part[3]))[0].astype(LOW))
    grad_up, grad_down = weights.reduce_mlp(hidden_two, grad_pre, activated, grad_mlp, flip)
    grad_hidden_two = total_parts([matmul_nt(g, part[2]) for g, part in zip(grad_pre, parts)])
    grad_middle = incoming + normalize_back(
        grad_hidden_two * (1.0 + pieces[4]), normed_two, inverse_two
    )
    grad_branch = (pieces[2] * grad_middle).astype(LOW)
    grad_out = weights.reduce_out(attended, grad_branch, flip)
    grad_attended = [matmul_nt(grad_branch, part[1]).astype(LOW) for part in parts]
    grad_qkv_rows = [mix_back(g, rows) for g, rows in zip(grad_attended, qkv)]
    grad_qkv = weights.reduce_qkv(hidden_one, grad_qkv_rows, flip)
    grad_hidden_one = total_parts(
        [matmul_nt(g, part[0]) for g, part in zip(grad_qkv_rows, parts)]
    )
    grad_residual = grad_middle + normalize_back(
        grad_hidden_one * (1.0 + pieces[1]), normed_one, inverse_one
    )
    sums = [
        jnp.sum(v.reshape(groups, -1, v.shape[-1]), axis=1)
        for v in (
            grad_hidden_one,
            grad_hidden_one * normed_one,
            grad_middle * branch,
            grad_hidden_two,
            grad_hidden_two * normed_two,
            incoming * mlp,
        )
    ]
    grad_mods = jnp.concatenate(sums, axis=-1)
    return grad_residual, grad_mods, (grad_qkv, grad_out, grad_up, grad_down)


def per_device(
    patch,
    seq,
    patch_axes,
    seq_axis,
    tokens,
    cotangent,
    class_ids,
    timesteps,
    segments,
    class_table,
    mod_spatial,
    qkv_spatial,
    out_spatial,
    up_spatial,
    down_spatial,
    mod_temporal,
    qkv_temporal,
    out_temporal,
    up_temporal,
    down_temporal,
):
    groups, frames, patch_rows, features = tokens.shape
    row_count = groups * frames * patch_rows
    head = features // HEADS
    hidden = up_spatial.shape[1] * seq
    grid = Grid(patch, seq, patch_axes, seq_axis)
    split = groups == 1 and Split.fits(patch, seq, frames, features, hidden)

    ways = max(1, patch // frames)
    subgroups = None
    if ways > 1:
        subgroups = [[a * ways + b for a in range(frames)] for b in range(ways)]

    def to_frames(array):
        moved = lax.all_to_all(
            array.reshape(groups, frames, patch_rows, features),
            patch_axes,
            split_axis=1,
            concat_axis=2,
            tiled=True,
            axis_index_groups=subgroups,
        )
        return moved.reshape(row_count, features)

    own_frames = max(1, frames // patch)

    def to_patches(array):
        moved = lax.all_to_all(
            array.reshape(groups, own_frames, -1, features),
            patch_axes,
            split_axis=2,
            concat_axis=1,
            tiled=True,
            axis_index_groups=subgroups,
        )
        return moved.reshape(row_count, features)

    def sharers(by):
        return [
            (a * ways + b, a * ways + (b + by) % ways)
            for a in range(patch // ways)
            for b in range(ways)
        ]

    def share_frame(array):
        if ways == 1:
            return array
        return jnp.concatenate(
            [array] + [lax.ppermute(array, patch_axes, sharers(j)) for j in range(1, ways)], axis=1
        )

    def share_frame_back(array):
        if ways == 1:
            return array
        cut = jnp.split(array, ways, axis=1)
        total = cut[0]
        for j in range(1, ways):
            total = total + lax.ppermute(cut[j], patch_axes, sharers(-j))
        return total

    whose = [jnp.stack([class_ids, timesteps])]
    whose += [grid.shift_x(whose[0], -j) for j in range(1, seq)]
    every_class = [w[0] for w in whose]
    conditions = []
    for chosen, times in whose:
        one_hot = (
            chosen[:, None] == jnp.arange(class_table.shape[0], dtype=jnp.int32)[None, :]
        ).astype(LOW)
        conditions.append(matmul(one_hot, class_table) + time_features(times, features))
    cond_low = [jax.nn.silu(c).astype(LOW) for c in conditions]
    mod_rows = features // patch
    first_row = grid.place * mod_rows
    cond_own = [lax.dynamic_slice_in_dim(c, first_row, mod_rows, axis=1) for c in cond_low]
    modulation = []

    def mod_steps(hold):
        together = jnp.concatenate(cond_own)
        mods = jnp.stack([matmul(together, mod_spatial), matmul(together, mod_temporal)], axis=1)
        for bit in grid.bits():
            mods = hold(mods + grid.xor_patch(mods, bit))
            yield
        mods = mods.reshape(seq, groups, 2, -1).transpose(0, 2, 1, 3)
        received = [mods[0]] + [grid.shift_x(mods[j], j) for j in range(1, seq)]
        ordered = in_order(received[:1] + received[:0:-1], grid.x)
        modulation.append(hold(jnp.concatenate(ordered, axis=-1)))
        yield

    width = mod_spatial.shape[1]

    def outer(columns):
        return lax.dot_general(
            jnp.concatenate(cond_own).astype(FULL),
            columns,
            (((0,), (0,)), ((), ())),
            precision=PRECISE,
            preferred_element_type=FULL,
        )

    def condition_part(columns, mod):
        return lax.dot_general(
            columns,
            mod.astype(FULL),
            (((1,), (1,)), ((), ())),
            precision=PRECISE,
            preferred_element_type=FULL,
        )

    def condition_steps(spatial_sums, temporal_sums, own_class):
        sums = jnp.stack([spatial_sums, temporal_sums])
        for bit in grid.bits():
            if split and bit == 1:
                continue
            sums = sums + (yield sums, partial(grid.xor_patch, bit=bit))
        sums = sums.reshape(2, groups, seq, width)
        columns = [pick(sums, 2, grid.x)]
        for j in range(1, seq):
            away = pick(sums, 2, (grid.x - j) % seq)
            columns.append((yield away, partial(grid.shift_x, by=-j)))
        columns = jnp.concatenate(columns, axis=1)
        parts = condition_part(columns[0], mod_spatial) + condition_part(columns[1], mod_temporal)
        parts = parts.reshape(seq, groups, mod_rows)
        total = parts
        for j in range(1, seq):
            total = total + jnp.roll((yield parts, partial(grid.shift_x, by=j)), j, axis=0)
        total = total[None]
        bit = 1
        while bit < patch:
            total = grid.join_patch(total, (yield total, partial(grid.xor_patch, bit=bit)), bit)
            bit *= 2
        grad_condition = total.transpose(1, 2, 0, 3).reshape(seq * groups, features)
        _, silu_back = jax.vjp(jax.nn.silu, jnp.concatenate(conditions))
        every_hot = (
            jnp.concatenate([own_class()] + every_class[1:])[:, None]
            == jnp.arange(class_table.shape[0], dtype=jnp.int32)[None, :]
        ).astype(FULL)
        grad_class_table = lax.dot_general(
            every_hot,
            silu_back(grad_condition)[0],
            (((0,), (0,)), ((), ())),
            precision=PRECISE,
            preferred_element_type=FULL,
        )
        yield grad_class_table, outer(columns[0]), outer(columns[1])

    def conditions_at_once(spatial_sums, temporal_sums):
        steps = condition_steps(spatial_sums, temporal_sums, lambda: class_ids)
        request = next(steps)
        while isinstance(request[1], partial):
            request = steps.send(request[1](request[0]))
        return request


    spatial_shards = (qkv_spatial, out_spatial, up_spatial, down_spatial)
    temporal_shards = (qkv_temporal, out_temporal, up_temporal, down_temporal)
    span = frames * patch_rows
    patch_of = jnp.arange(span, dtype=jnp.int32) % patch_rows
    place_of = jnp.repeat(segments, patch_rows, axis=1) * patch_rows + patch_of[None, :]

    if split:
        plan = Split(grid, head, hidden // patch, whose[0])
        hold = plan.tie
        marks = (place_of.reshape(-1, 1), place_of.reshape(1, -1))
        early = plan.fly(tokens, to_frames)
        shards = plan.prepare(spatial_shards, temporal_shards)
        steps = mod_steps(hold)
        for _ in range(2):
            next(steps)

        plan.land(early)

        def mods_of():
            return [
                jnp.pad(modulation[-1][block].reshape(6, features), ((0, 2), (0, 0)))
                for block in range(2)
            ]

        result, spatial_state, temporal_state = plan.forward(
            early.value,
            mods_of,
            steps,
            shards,
            down_spatial.shape,
            marks,
            to_frames,
            to_patches,
        )
        out_tokens = result.reshape(tokens.shape)
        grad_spatial_in, condition_grads, spatial_grads, temporal_grads = plan.backward(
            spatial_state,
            temporal_state,
            cotangent.reshape(row_count, features),
            to_frames,
            to_patches,
            lambda s, t: condition_steps(s, t, lambda: plan.token[0]),
        )
        grad_tokens = grad_spatial_in.astype(FULL).reshape(tokens.shape)
    else:
        weights = WholeWeights(grid, features, hidden)
        list(mod_steps(lambda v: v))

        def pieces_of(block):
            rows = modulation[-1][block]
            if groups > 1:
                rows = jnp.repeat(rows, row_count // groups, axis=0)
            return [rows[:, k * features : (k + 1) * features] for k in range(6)]

        spatial_pieces, temporal_pieces = pieces_of(0), pieces_of(1)
        spatial_parts, temporal_parts = weights.fetch(spatial_shards, temporal_shards)
        same = (place_of[:, :, None] == place_of[:, None, :])[:, None, :, :]
        itself = lambda array: array
        spatial_batch = groups * own_frames
        spatial_mix = lambda rows: attend(rows, spatial_batch, None, head, share_frame)
        spatial_mix_back = lambda g, rows: attend_back(
            g, rows, spatial_batch, None, head, share_frame, share_frame_back
        )
        temporal_mix = lambda rows: attend(rows, groups, same, head, itself)
        temporal_mix_back = lambda g, rows: attend_back(
            g, rows, groups, same, head, itself, itself
        )
        spatial_in = to_frames(tokens).astype(FULL)
        spatial_out, spatial_saved = block_forward(
            spatial_in, spatial_pieces, spatial_parts, spatial_mix
        )
        temporal_in = to_patches(spatial_out.astype(LOW)).astype(FULL)
        result, temporal_saved = block_forward(
            temporal_in, temporal_pieces, temporal_parts, temporal_mix
        )
        out_tokens = result.astype(LOW).reshape(tokens.shape)
        incoming = cotangent.astype(FULL).reshape(row_count, features)
        grad_temporal_in, temporal_sums, temporal_grads = block_backward(
            incoming,
            temporal_pieces,
            temporal_parts,
            temporal_saved,
            temporal_mix_back,
            weights,
            groups,
            True,
        )
        grad_spatial_out = to_frames(grad_temporal_in.astype(LOW)).astype(FULL)
        grad_spatial_in, spatial_sums, spatial_grads = block_backward(
            grad_spatial_out,
            spatial_pieces,
            spatial_parts,
            spatial_saved,
            spatial_mix_back,
            weights,
            groups,
            False,
        )
        grad_tokens = to_patches(grad_spatial_in.astype(LOW)).astype(FULL).reshape(tokens.shape)
        condition_grads = conditions_at_once(spatial_sums, temporal_sums)

    grad_class_table, grad_mod_spatial, grad_mod_temporal = condition_grads

    return (
        out_tokens,
        grad_tokens,
        grad_class_table,
        grad_mod_spatial,
        *spatial_grads,
        grad_mod_temporal,
        *temporal_grads,
    )


def solution(mesh):
    patch, seq = mesh.shape["patch"], mesh.shape["seq"]
    patch_axes, seq_axis = "patch", "seq"
    if seq == 2 and patch % 4 == 0:
        patch_axes, seq_axis = ("z", "y", "core"), "x"
        mesh = Mesh(mesh.devices.reshape(patch // 4, 2, 2, seq), patch_axes + (seq_axis,))
    rows = P(seq_axis, None, patch_axes, None)
    both = P(patch_axes, seq_axis)
    return jax.shard_map(
        partial(per_device, patch, seq, patch_axes, seq_axis),
        mesh=mesh,
        in_specs=(rows, rows, P(seq_axis), P(seq_axis), P(seq_axis, None), P()) + (both,) * 10,
        out_specs=(rows, rows, P()) + (both,) * 10,
        check_vma=False,
    )
```
